32 devices in a mesh: clip: 4 (over z), seq: 8 (over y, x, core).
Axes of the slice: x: 2, y: 2, z: 4, core: 2. Of those that a mesh axis runs over, the one named last changes fastest.
Arguments:
- tokens: bfloat16 [4, 16, 256, 1152], P('clip', 'seq'), may hold values from -4 to 4
- text: bfloat16 [4, 120, 1152], P('clip'), may hold values from -4 to 4
- timesteps: int32 [4], replicated, may hold values from 0 to 999
- text_counts: int32 [4], P('clip'), may hold values from 1 to 120
- out_grad: bfloat16 [4, 16, 256, 1152], P('clip', 'seq'), may hold values from -3 to 3
- time_weight: bfloat16 [1152, 6912], P(('clip', 'seq')), may hold values from -0.1875 to 0.1875
- s_qkv: bfloat16 [1, 1152, 3456], P(None, ('clip', 'seq')), may hold values from -0.1875 to 0.1875
- s_proj: bfloat16 [1, 1152, 1152], P(None, ('clip', 'seq')), may hold values from -0.75 to 0.75
- t_qkv: bfloat16 [1, 1152, 3456], P(None, ('clip', 'seq')), may hold values from -0.09375 to 0.09375
- t_proj: bfloat16 [1, 1152, 1152], P(None, ('clip', 'seq')), may hold values from -0.75 to 0.75
- c_query: bfloat16 [1, 1152, 1152], P(None, ('clip', 'seq')), may hold values from -0.09375 to 0.09375
- c_kv: bfloat16 [1, 1152, 2304], P(None, ('clip', 'seq')), may hold values from -0.1875 to 0.1875
- c_proj: bfloat16 [1, 1152, 1152], P(None, ('clip', 'seq')), may hold values from -0.5 to 0.5
- mlp_in: bfloat16 [1, 1152, 4608], P(None, ('clip', 'seq')), may hold values from -0.1875 to 0.1875
- mlp_out: bfloat16 [1, 4608, 1152], P(None, ('clip', 'seq')), may hold values from -0.09375 to 0.09375
- vectors: bfloat16 [1, 20, 1152], P(None, None, ('clip', 'seq')), may hold values from -1.75 to 1.75
Outputs:
- output: float32 [4, 16, 256, 1152], P('clip', 'seq')
- token_grad: float32 [4, 16, 256, 1152], P('clip', 'seq')
- text_grad: float32 [4, 120, 1152], P('clip', None, 'seq')
- time_weight_grad: float32 [1152, 6912], P(('clip', 'seq'))
- s_qkv_grad: float32 [1, 1152, 3456], P(None, ('clip', 'seq'))
- s_proj_grad: float32 [1, 1152, 1152], P(None, ('clip', 'seq'))
- t_qkv_grad: float32 [1, 1152, 3456], P(None, ('clip', 'seq'))
- t_proj_grad: float32 [1, 1152, 1152], P(None, ('clip', 'seq'))
- c_query_grad: float32 [1, 1152, 1152], P(None, ('clip', 'seq'))
- c_kv_grad: float32 [1, 1152, 2304], P(None, ('clip', 'seq'))
- c_proj_grad: float32 [1, 1152, 1152], P(None, ('clip', 'seq'))
- mlp_in_grad: float32 [1, 1152, 4608], P(None, ('clip', 'seq'))
- mlp_out_grad: float32 [1, 4608, 1152], P(None, ('clip', 'seq'))
- vectors_grad: float32 [1, 20, 1152], P(None, None, ('clip', 'seq'))
The draws below stay inside these ranges and needn't reach their ends.
Inputs may be any that keep to these rules, and one draw needn't show every extreme that they name: Each clip's caption is its first text_counts tokens; the rest are padding.
All inputs are finite; a program needn't handle non-finite values.
Results may differ from the reference program's by a relative error of at most 0.03.
Values may be sent and summed in bfloat16 or wider, within the bound.
A program may use at most 576 MiB of HBM per device.

```python
import math
import jax
import jax.numpy as jnp
from jax import lax

D = 1152
HEADS = 16
FF = 4608
TEXT = 120
FRAMES = 16
PATCHES = 256
LAYERS = 1
HEAD_DIM = 72
NVEC = 20
CLIPS = 4


def unit_field(key, shape):
    values = jnp.clip(jax.random.normal(key, shape, jnp.float32), -4.0, 4.0)
    return values


def draw_tokens(key, part):
    key = jax.random.fold_in(key, 11)
    return unit_field(key, (CLIPS, FRAMES, PATCHES, D)).astype(jnp.bfloat16)


def draw_text(key, part):
    key = jax.random.fold_in(key, 23)
    return unit_field(key, (CLIPS, TEXT, D)).astype(jnp.bfloat16)


def set_ends(entries, rng, least, high):
    dims = entries.shape
    index_at = [jax.random.randint(jax.random.fold_in(rng, axis), (), 0, dims[axis]) for axis in range(len(dims))]
    entries = entries.at[tuple(index_at)].set(least)
    longest = dims.index(max(dims))
    index_at[longest] = (index_at[longest] + 1) % dims[longest]
    return entries.at[tuple(index_at)].set(high)


def levels(stream_key, shape, shards, least, top_value):
    gain, own = 1.0, jax.random.fold_in(stream_key, 6)
    for axis_at, blocks in shards:
        draws = jnp.exp(jax.random.uniform(jax.random.fold_in(own, axis_at), (blocks,), jnp.float32, least / len(shards), top_value / len(shards)))
        gain = gain * jnp.repeat(draws, shape[axis_at] // blocks).reshape([-1 if axis == axis_at else 1 for axis in range(len(shape))])
    return gain


def normal_values(key, shape, deviation, most, pieces=(), kind=jnp.bfloat16):
    values = deviation * jax.random.normal(key, shape, jnp.float32)
    if pieces:
        values = values * levels(key, shape, pieces, -0.22, 0.18)
    return jnp.clip(values, -most, most).astype(kind)


def setup_inputs(seed: int = 0) -> dict:
    keys = jax.random.split(jax.random.key(seed), 17)
    return {
        "tokens": draw_tokens(jax.random.fold_in(keys[16], 71), 0),
        "text": draw_text(jax.random.fold_in(keys[16], 71), 0),
        "timesteps": set_ends(jax.random.randint(keys[2], (CLIPS,), 0, 1000), jax.random.fold_in(keys[2], 1), 0, 999).astype(jnp.int32),
        "text_counts": set_ends(jax.random.randint(keys[3], (CLIPS,), 1, TEXT + 1), jax.random.fold_in(keys[3], 1), 1, TEXT).astype(jnp.int32),
        "out_grad": normal_values(keys[4], (CLIPS, FRAMES, PATCHES, D), 0.5, 3.0, ((0, 4), (1, 8))),
        "time_weight": normal_values(keys[5], (D, 6 * D), D ** -0.5, 0.1875, ((0, 32),)),
        "s_qkv": normal_values(keys[6], (LAYERS, D, 3 * D), D ** -0.5, 0.1875, ((1, 32),)),
        "s_proj": normal_values(keys[7], (LAYERS, D, D), (D // 16) ** -0.5, 0.75, ((1, 32),)),
        "t_qkv": normal_values(keys[8], (LAYERS, D, 3 * D), (4 * D) ** -0.5, 0.09375, ((1, 32),)),
        "t_proj": normal_values(keys[9], (LAYERS, D, D), (D // 16) ** -0.5, 0.75, ((1, 32),)),
        "c_query": normal_values(keys[10], (LAYERS, D, D), (4 * D) ** -0.5, 0.09375, ((1, 32),)),
        "c_kv": normal_values(keys[11], (LAYERS, D, 2 * D), D ** -0.5, 0.1875, ((1, 32),)),
        "c_proj": normal_values(keys[12], (LAYERS, D, D), (D // 8) ** -0.5, 0.5, ((1, 32),)),
        "mlp_in": normal_values(keys[13], (LAYERS, D, FF), D ** -0.5, 0.1875, ((1, 32),)),
        "mlp_out": normal_values(keys[14], (LAYERS, FF, D), FF ** -0.5, 0.09375, ((1, 32),)),
        "vectors": normal_values(keys[15], (LAYERS, NVEC, D), 0.3, 1.75, ((2, 32),)),
    }


EPSILON = 1e-06
HIGHEST = lax.Precision.HIGHEST

@jax.custom_vjp
def low(v):
    return lax.optimization_barrier(v.astype(jnp.bfloat16)).astype(jnp.float32)

@jax.custom_vjp
def low_back(v):
    return v

def low_keep(v):
    return (low(v), None)

def low_pass(kept, grad):
    return (grad,)

def back_keep(v):
    return (v, None)

def back_low(kept, grad):
    return (low(grad),)
low.defvjp(low_keep, low_pass)
low_back.defvjp(back_keep, back_low)

def matmul_high(left_arr, right_arr):
    return jnp.dot(left_arr, right_arr, precision=HIGHEST)

def timestep_embed(step_values):
    half_width = D // 2
    frequency = jnp.exp(-math.log(10000.0) * jnp.arange(half_width, dtype=jnp.float32) / half_width)
    angles = step_values.astype(jnp.float32)[:, None] * frequency[None, :]
    return jnp.concatenate([jnp.cos(angles), jnp.sin(angles)], axis=-1)

def layer_norm(rows_in):
    centered = rows_in - lax.optimization_barrier(jnp.mean(rows_in, axis=-1, keepdims=True))
    return centered * lax.rsqrt(lax.optimization_barrier(jnp.mean(centered * centered, axis=-1, keepdims=True)) + EPSILON)

def split_heads(packed_arr):
    return packed_arr.reshape(packed_arr.shape[:-1] + (HEADS, HEAD_DIM))

def merge_heads(head_arr):
    return head_arr.reshape(head_arr.shape[:-2] + (D,))

def attend(queries, key_rows, values, key_mask):
    scores = jnp.einsum('...qhe,...khe->...hqk', queries, key_rows, precision=HIGHEST) * HEAD_DIM ** (-0.5)
    scores = low_back(jnp.where(key_mask, scores, -1000000000.0))
    shifted = scores - lax.optimization_barrier(jnp.max(scores, axis=-1, keepdims=True))
    exp_scores = jnp.exp(shifted)
    attn_probs = exp_scores / lax.optimization_barrier(jnp.sum(exp_scores, axis=-1, keepdims=True))
    mixed_heads = jnp.einsum('...hqk,...khe->...qhe', low(attn_probs), values, precision=HIGHEST)
    return low_back(low(merge_heads(mixed_heads)))

def self_attention(inputs, qkv_weight, query_bias, value_bias, proj_weight, proj_bias, key_mask):
    bias_row = jnp.concatenate([query_bias, jnp.zeros_like(query_bias), value_bias])
    packed = low_back(low(matmul_high(inputs, qkv_weight) + bias_row))
    queries = split_heads(packed[..., :D])
    key_rows = split_heads(packed[..., D:2 * D])
    values = split_heads(packed[..., 2 * D:])
    mixed_out = attend(queries, key_rows, values, key_mask)
    return matmul_high(mixed_out, proj_weight) + proj_bias

def stdit_block(hidden, text_rows, text_mask, mod_table, vector_rows, weights):
    s_qkv, s_proj, t_qkv, t_proj, c_query, c_kv, c_proj, mlp_in, mlp_out = weights
    patch_mask = jnp.ones((PATCHES,), dtype=jnp.bool_)
    frame_mask = jnp.ones((FRAMES,), dtype=jnp.bool_)
    normed = low(layer_norm(hidden) * (1.0 + mod_table[1]) + mod_table[0])
    spatial = low_back(self_attention(normed, s_qkv, vector_rows[0], vector_rows[1], s_proj, vector_rows[2], patch_mask))
    hidden = hidden + mod_table[2] * spatial
    moved = low_back(low(jnp.swapaxes(hidden, 0, 1)))
    temporal = low_back(low(self_attention(moved, t_qkv, vector_rows[3], vector_rows[4], t_proj, vector_rows[5], frame_mask)))
    hidden = hidden + mod_table[2] * jnp.swapaxes(temporal, 0, 1)
    cross_in = low(hidden).reshape(FRAMES * PATCHES, D)
    queries = split_heads(low_back(low(matmul_high(cross_in, c_query) + vector_rows[6])))
    kv_bias = jnp.concatenate([jnp.zeros_like(vector_rows[7]), vector_rows[7]])
    packed = low_back(low(matmul_high(text_rows, c_kv) + kv_bias))
    mixed_out = attend(queries, split_heads(packed[:, :D]), split_heads(packed[:, D:]), text_mask)
    cross = low_back(matmul_high(mixed_out, c_proj) + vector_rows[8])
    hidden = hidden + cross.reshape(FRAMES, PATCHES, D)
    normed_two = low(layer_norm(hidden) * (1.0 + mod_table[4]) + mod_table[3])
    inner_act = low_back(matmul_high(normed_two, mlp_in) + vector_rows[16:].reshape(FF))
    gelu_out = low(jax.nn.gelu(inner_act, approximate=True))
    mlp_branch = low_back(matmul_high(gelu_out, mlp_out) + vector_rows[9])
    return hidden + mod_table[5] * mlp_branch

def clip_forward(clip_tokens, clip_text, text_count, step_value, params):
    time_embed = low(jax.nn.silu(timestep_embed(step_value[None])))
    modulation = matmul_high(time_embed, params[0]).reshape(6, D)
    text_mask = jnp.arange(TEXT) < text_count
    hidden = clip_tokens
    for layer_idx in range(LAYERS):
        vector_rows = params[10][layer_idx]
        mod_table = modulation + vector_rows[10:16]
        layer_weights = tuple((weight[layer_idx] for weight in params[1:10]))
        hidden = stdit_block(hidden, clip_text, text_mask, mod_table, vector_rows, layer_weights)
    return hidden

def reference(tokens, text, timesteps, text_counts, out_grad, time_weight, s_qkv, s_proj, t_qkv, t_proj, c_query, c_kv, c_proj, mlp_in, mlp_out, vectors):
    params = tuple((weight.astype(jnp.float32) for weight in (time_weight, s_qkv, s_proj, t_qkv, t_proj, c_query, c_kv, c_proj, mlp_in, mlp_out, vectors)))

    def forward(tokens_f, text_f, params_f):

        def one_clip(clip_args):
            clip_tokens, clip_text, text_count, step_value = clip_args
            return clip_forward(clip_tokens, clip_text, text_count, step_value, params_f)
        return lax.map(jax.checkpoint(one_clip), (tokens_f, text_f, text_counts, timesteps))
    result, pullback = jax.vjp(forward, tokens.astype(jnp.float32), text.astype(jnp.float32), params)
    token_grad, text_grad, grads = pullback(out_grad.astype(jnp.float32))
    return (result, token_grad, text_grad, grads[0], grads[1], grads[2], grads[3], grads[4], grads[5], grads[6], grads[7], grads[8], grads[9], grads[10])
```

```python
from functools import partial
import math

import jax
import jax.numpy as jnp
from jax import lax
from jax.sharding import PartitionSpec as P

HEADS = 16


EPSILON = 1e-06
HIGHEST = lax.Precision.HIGHEST
SPATIAL = ("bqhe", "bkhe", "bhqk")
TEMPORAL = ("cqphe", "ckphe", "cphqk")
CROSS = ("cqhe", "ckhe", "chqk")


def product(left_arr, right_arr):
    return lax.dot_general(
        left_arr,
        right_arr,
        (((left_arr.ndim - 1,), (0,)), ((), ())),
        preferred_element_type=jnp.float32,
    )


def product_back(grad_arr, weight):
    return lax.dot_general(
        grad_arr,
        weight,
        (((grad_arr.ndim - 1,), (1,)), ((), ())),
        preferred_element_type=jnp.float32,
    )


def outer_sum(left_arr, right_arr):
    left_rows = left_arr.reshape(-1, left_arr.shape[-1])
    right_rows = right_arr.reshape(-1, right_arr.shape[-1])
    return lax.dot_general(
        left_rows, right_rows, (((0,), (0,)), ((), ())), preferred_element_type=jnp.float32
    )


def column_sum(grad_arr):
    return jnp.sum(grad_arr.astype(jnp.float32).reshape(-1, grad_arr.shape[-1]), axis=0)


def timestep_embed(step_values, model_width):
    half_width = model_width // 2
    frequency = jnp.exp(-math.log(10000.0) * jnp.arange(half_width, dtype=jnp.float32) / half_width)
    angles = step_values.astype(jnp.float32)[:, None] * frequency[None, :]
    return jnp.concatenate([jnp.cos(angles), jnp.sin(angles)], axis=-1)


def modulate(hidden, shift_row, scale_row):
    centered = hidden - jnp.mean(hidden, axis=-1, keepdims=True)
    normed = centered * lax.rsqrt(jnp.mean(centered * centered, axis=-1, keepdims=True) + EPSILON)
    return normed * (1.0 + scale_row[:, None, :]) + shift_row[:, None, :]


def split_heads(packed_arr, heads):
    return packed_arr.reshape(packed_arr.shape[:-1] + (heads, packed_arr.shape[-1] // heads))


def merge_heads(head_arr):
    return head_arr.reshape(head_arr.shape[:-2] + (head_arr.shape[-2] * head_arr.shape[-1],))


def attend_scores(queries, key_rows, key_mask, forms):
    query_form, key_form, score_form = forms
    scale_factor = queries.shape[-1] ** (-0.5)
    scores = (
        jnp.einsum(
            query_form + "," + key_form + "->" + score_form,
            queries,
            key_rows,
            preferred_element_type=jnp.float32,
        )
        * scale_factor
    )
    if key_mask is not None:
        scores = jnp.where(key_mask, scores, -1000000000.0)
    return scores


def attend_forward(queries, key_rows, values, key_mask, forms):
    query_form, key_form, score_form = forms
    scores = attend_scores(queries, key_rows, key_mask, forms)
    top_score = jnp.max(scores, axis=-1, keepdims=True)
    log_total = top_score + jnp.log(jnp.sum(jnp.exp(scores - top_score), axis=-1, keepdims=True))
    attn_probs = jnp.exp(scores - log_total).astype(jnp.bfloat16)
    mixed_heads = jnp.einsum(
        score_form + "," + key_form + "->" + query_form,
        attn_probs,
        values,
        preferred_element_type=jnp.float32,
    )
    return (mixed_heads.astype(jnp.bfloat16), log_total)


def attend_backward(queries, key_rows, values, key_mask, log_total, grad_mixed, forms):
    query_form, key_form, score_form = forms
    scale_factor = queries.shape[-1] ** (-0.5)
    scores = attend_scores(queries, key_rows, key_mask, forms)
    attn_probs = jnp.exp(scores - log_total)
    grad_probs = jnp.einsum(
        query_form + "," + key_form + "->" + score_form,
        grad_mixed,
        values,
        preferred_element_type=jnp.float32,
    )
    inner_dot = jnp.sum(attn_probs * grad_probs, axis=-1, keepdims=True)
    grad_scores = (attn_probs * (grad_probs - inner_dot)).astype(jnp.bfloat16)
    grad_values = jnp.einsum(
        score_form + "," + query_form + "->" + key_form,
        attn_probs.astype(jnp.bfloat16),
        grad_mixed,
        preferred_element_type=jnp.float32,
    )
    grad_queries = (
        jnp.einsum(
            score_form + "," + key_form + "->" + query_form,
            grad_scores,
            key_rows,
            preferred_element_type=jnp.float32,
        )
        * scale_factor
    )
    grad_keys = (
        jnp.einsum(
            score_form + "," + query_form + "->" + key_form,
            grad_scores,
            queries,
            preferred_element_type=jnp.float32,
        )
        * scale_factor
    )
    return (grad_queries, grad_keys, grad_values)


def project_qkv(inputs, weight, query_bias, value_bias, heads):
    model_width = query_bias.shape[0]
    bias_row = jnp.concatenate([query_bias, jnp.zeros_like(query_bias), value_bias]).astype(
        jnp.float32
    )
    packed = (product(inputs, weight) + bias_row).astype(jnp.bfloat16)
    return (
        split_heads(packed[..., :model_width], heads),
        split_heads(packed[..., model_width : 2 * model_width], heads),
        split_heads(packed[..., 2 * model_width :], heads),
    )


def qkv_backward(grad_parts, inputs, weight):
    model_width = weight.shape[0]
    packed_grad = jnp.concatenate(
        [merge_heads(grad_part) for grad_part in grad_parts], axis=-1
    ).astype(jnp.bfloat16)
    return (
        outer_sum(inputs, packed_grad),
        product_back(packed_grad, weight),
        column_sum(packed_grad[..., :model_width]),
        column_sum(packed_grad[..., 2 * model_width :]),
    )


def layer_forward(hidden, layer_mats, modulation, text, text_mask, heads, frame_count):
    w_sqkv, w_sproj, w_tqkv, w_tproj, w_cquery, w_ckv, w_cproj, w_in, w_out, vec_rows = layer_mats
    clip_count, row_count, model_width = hidden.shape
    patch_count = row_count // frame_count
    vec_float = vec_rows.astype(jnp.float32)
    mod_table = modulation + vec_float[10:16][None]
    gate_one = mod_table[:, None, 2]
    normed = (
        modulate(hidden, mod_table[:, 0], mod_table[:, 1])
        .astype(jnp.bfloat16)
        .reshape(clip_count * frame_count, patch_count, model_width)
    )
    s_query, s_key, s_value = project_qkv(normed, w_sqkv, vec_rows[0], vec_rows[1], heads)
    s_mixed, s_total = attend_forward(s_query, s_key, s_value, None, SPATIAL)
    s_flat = merge_heads(s_mixed)
    s_branch = (product(s_flat, w_sproj) + vec_float[2]).reshape(clip_count, row_count, model_width)
    hidden_one = hidden + gate_one * s_branch
    frames_view = hidden_one.astype(jnp.bfloat16).reshape(
        clip_count, frame_count, patch_count, model_width
    )
    moved = lax.all_to_all(frames_view, "seq", split_axis=2, concat_axis=1, tiled=True)
    t_query, t_key, t_value = project_qkv(moved, w_tqkv, vec_rows[3], vec_rows[4], heads)
    t_mixed, t_total = attend_forward(t_query, t_key, t_value, None, TEMPORAL)
    t_flat = merge_heads(t_mixed)
    t_branch = (product(t_flat, w_tproj) + vec_float[5]).astype(jnp.bfloat16)
    t_back = lax.all_to_all(t_branch, "seq", split_axis=1, concat_axis=2, tiled=True).reshape(
        clip_count, row_count, model_width
    )
    hidden_two = hidden_one + gate_one * t_back.astype(jnp.float32)
    cross_in = hidden_two.astype(jnp.bfloat16)
    c_query = split_heads((product(cross_in, w_cquery) + vec_float[6]).astype(jnp.bfloat16), heads)
    kv_bias = jnp.concatenate([jnp.zeros_like(vec_float[7]), vec_float[7]])
    c_packed = (product(text, w_ckv) + kv_bias).astype(jnp.bfloat16)
    c_key = split_heads(c_packed[..., :model_width], heads)
    c_value = split_heads(c_packed[..., model_width:], heads)
    c_mixed, c_total = attend_forward(c_query, c_key, c_value, text_mask, CROSS)
    c_flat = merge_heads(c_mixed)
    hidden_three = hidden_two + (product(c_flat, w_cproj) + vec_float[8])
    normed_two = modulate(hidden_three, mod_table[:, 3], mod_table[:, 4]).astype(jnp.bfloat16)
    inner_act = product(normed_two, w_in) + vec_float[16:].reshape(-1)
    gelu_out = jax.nn.gelu(inner_act, approximate=True).astype(jnp.bfloat16)
    mlp_branch = product(gelu_out, w_out) + vec_float[9]
    hidden_four = hidden_three + mod_table[:, None, 5] * mlp_branch
    saved = dict(
        mod_table=mod_table,
        hidden=hidden,
        normed=normed,
        s_query=s_query,
        s_key=s_key,
        s_value=s_value,
        s_total=s_total,
        s_flat=s_flat,
        s_branch=s_branch,
        moved=moved,
        t_query=t_query,
        t_key=t_key,
        t_value=t_value,
        t_total=t_total,
        t_flat=t_flat,
        t_back=t_back,
        cross_in=cross_in,
        c_query=c_query,
        c_key=c_key,
        c_value=c_value,
        c_total=c_total,
        c_flat=c_flat,
        hidden_three=hidden_three,
        normed_two=normed_two,
        inner_act=inner_act,
        gelu_out=gelu_out,
        mlp_branch=mlp_branch,
    )
    return (hidden_four, saved)


def layer_backward(grad_hidden, saved, layer_mats, text, text_mask, heads, frame_count):
    w_sqkv, w_sproj, w_tqkv, w_tproj, w_cquery, w_ckv, w_cproj, w_in, w_out, vec_rows = layer_mats
    clip_count, row_count, model_width = grad_hidden.shape
    patch_count = row_count // frame_count
    mod_table = saved["mod_table"]
    gate_one = mod_table[:, None, 2]
    gate_two = mod_table[:, None, 5]
    grad_mlp = (grad_hidden * gate_two).astype(jnp.bfloat16)
    grad_gate_two = jnp.sum(grad_hidden * saved["mlp_branch"], axis=1)
    grad_w_out = outer_sum(saved["gelu_out"], grad_mlp)
    bias_out = column_sum(grad_mlp)
    grad_gelu = product_back(grad_mlp, w_out)
    gelu_pull = jax.vjp(partial(jax.nn.gelu, approximate=True), saved["inner_act"])[1]
    grad_inner = gelu_pull(grad_gelu)[0].astype(jnp.bfloat16)
    grad_w_in = outer_sum(saved["normed_two"], grad_inner)
    bias_in = column_sum(grad_inner)
    grad_normed_two = product_back(grad_inner, w_in)
    norm_pull = jax.vjp(modulate, saved["hidden_three"], mod_table[:, 3], mod_table[:, 4])[1]
    grad_three, grad_shift_two, grad_scale_two = norm_pull(grad_normed_two)
    grad_three = grad_hidden + grad_three
    grad_cross = grad_three.astype(jnp.bfloat16)
    grad_w_cproj = outer_sum(saved["c_flat"], grad_cross)
    bias_cproj = column_sum(grad_cross)
    grad_cmixed = split_heads(product_back(grad_cross, w_cproj).astype(jnp.bfloat16), heads)
    cq_grad, ck_grad, cv_grad = attend_backward(
        saved["c_query"],
        saved["c_key"],
        saved["c_value"],
        text_mask,
        saved["c_total"],
        grad_cmixed,
        CROSS,
    )
    grad_cquery = merge_heads(cq_grad).astype(jnp.bfloat16)
    grad_w_cquery = outer_sum(saved["cross_in"], grad_cquery)
    bias_cquery = column_sum(grad_cquery)
    grad_two = grad_three + product_back(grad_cquery, w_cquery)
    grad_kv = jnp.concatenate([merge_heads(ck_grad), merge_heads(cv_grad)], axis=-1).astype(
        jnp.bfloat16
    )
    grad_w_ckv = outer_sum(text, grad_kv)
    bias_cvalue = column_sum(grad_kv[..., model_width:])
    text_part = product_back(grad_kv, w_ckv)
    grad_gate_one = jnp.sum(grad_two * saved["t_back"].astype(jnp.float32), axis=1)
    grad_temporal = (
        (grad_two * gate_one)
        .astype(jnp.bfloat16)
        .reshape(clip_count, frame_count, patch_count, model_width)
    )
    grad_places = lax.all_to_all(grad_temporal, "seq", split_axis=2, concat_axis=1, tiled=True)
    grad_w_tproj = outer_sum(saved["t_flat"], grad_places)
    bias_tproj = column_sum(grad_places)
    grad_tmixed = split_heads(product_back(grad_places, w_tproj).astype(jnp.bfloat16), heads)
    temporal_grads = attend_backward(
        saved["t_query"],
        saved["t_key"],
        saved["t_value"],
        None,
        saved["t_total"],
        grad_tmixed,
        TEMPORAL,
    )
    grad_w_tqkv, grad_moved, bias_tquery, bias_tvalue = qkv_backward(
        temporal_grads, saved["moved"], w_tqkv
    )
    grad_frames = lax.all_to_all(
        grad_moved.astype(jnp.bfloat16), "seq", split_axis=1, concat_axis=2, tiled=True
    )
    grad_one = grad_two + grad_frames.astype(jnp.float32).reshape(
        clip_count, row_count, model_width
    )
    grad_gate_one = grad_gate_one + jnp.sum(grad_one * saved["s_branch"], axis=1)
    grad_spatial = (
        (grad_one * gate_one)
        .astype(jnp.bfloat16)
        .reshape(clip_count * frame_count, patch_count, model_width)
    )
    grad_w_sproj = outer_sum(saved["s_flat"], grad_spatial)
    bias_sproj = column_sum(grad_spatial)
    grad_smixed = split_heads(product_back(grad_spatial, w_sproj).astype(jnp.bfloat16), heads)
    spatial_grads = attend_backward(
        saved["s_query"],
        saved["s_key"],
        saved["s_value"],
        None,
        saved["s_total"],
        grad_smixed,
        SPATIAL,
    )
    grad_w_sqkv, grad_normed, bias_squery, bias_svalue = qkv_backward(
        spatial_grads, saved["normed"], w_sqkv
    )
    first_pull = jax.vjp(modulate, saved["hidden"], mod_table[:, 0], mod_table[:, 1])[1]
    grad_zero, grad_shift_one, grad_scale_one = first_pull(
        grad_normed.reshape(clip_count, row_count, model_width)
    )
    grad_input = grad_one + grad_zero
    grad_table = jnp.stack(
        [
            grad_shift_one,
            grad_scale_one,
            grad_gate_one,
            grad_shift_two,
            grad_scale_two,
            grad_gate_two,
        ],
        axis=1,
    )
    bias_rows = jnp.stack(
        [
            bias_squery,
            bias_svalue,
            bias_sproj,
            bias_tquery,
            bias_tvalue,
            bias_tproj,
            bias_cquery,
            bias_cvalue,
            bias_cproj,
            bias_out,
        ]
    )
    vec_grad = jnp.concatenate(
        [bias_rows, jnp.sum(grad_table, axis=0), bias_in.reshape(-1, model_width)], axis=0
    )
    layer_grads = (
        grad_w_sqkv,
        grad_w_sproj,
        grad_w_tqkv,
        grad_w_tproj,
        grad_w_cquery,
        grad_w_ckv,
        grad_w_cproj,
        grad_w_in,
        grad_w_out,
        vec_grad,
    )
    return (grad_input, layer_grads, text_part, grad_table)


def per_device(
    tokens,
    text,
    timesteps,
    text_counts,
    out_grad,
    time_weight,
    s_qkv,
    s_proj,
    t_qkv,
    t_proj,
    c_query,
    c_kv,
    c_proj,
    mlp_in,
    mlp_out,
    vectors,
):
    clip_count, frame_count, patch_count, model_width = tokens.shape
    layer_count = s_qkv.shape[0]
    heads = HEADS
    clip_first = lax.axis_index("clip") * clip_count
    my_steps = lax.dynamic_slice_in_dim(timesteps, clip_first, clip_count)
    time_embed = jax.nn.silu(timestep_embed(my_steps, model_width)).astype(jnp.bfloat16)
    time_full = lax.all_gather(time_weight, ("clip", "seq"), axis=0, tiled=True)
    modulation = product(time_embed, time_full).reshape(clip_count, 6, model_width)
    text_mask = (jnp.arange(text.shape[1])[None, :] < text_counts[:, None])[:, None, None, :]
    hidden = tokens.astype(jnp.float32).reshape(clip_count, frame_count * patch_count, model_width)
    layer_mats = None
    layer_idx = 0
    layer_mats = (
        lax.all_gather(s_qkv[layer_idx], ("clip", "seq"), axis=0, tiled=True),
        lax.all_gather(s_proj[layer_idx], ("clip", "seq"), axis=0, tiled=True),
        lax.all_gather(t_qkv[layer_idx], ("clip", "seq"), axis=0, tiled=True),
        lax.all_gather(t_proj[layer_idx], ("clip", "seq"), axis=0, tiled=True),
        lax.all_gather(c_query[layer_idx], ("clip", "seq"), axis=0, tiled=True),
        lax.all_gather(c_kv[layer_idx], ("clip", "seq"), axis=0, tiled=True),
        lax.all_gather(c_proj[layer_idx], ("clip", "seq"), axis=0, tiled=True),
        lax.all_gather(mlp_in[layer_idx], ("clip", "seq"), axis=0, tiled=True),
        lax.all_gather(mlp_out[layer_idx], ("clip", "seq"), axis=0, tiled=True),
        lax.all_gather(vectors[layer_idx], ("clip", "seq"), axis=1, tiled=True),
    )
    hidden, saved = layer_forward(
        hidden, layer_mats, modulation, text, text_mask, heads, frame_count
    )
    saved_list = [saved]
    output = hidden.reshape(tokens.shape)
    grad_hidden = out_grad.astype(jnp.float32).reshape(hidden.shape)
    grad_text = jnp.zeros(text.shape, jnp.float32)
    grad_mod = jnp.zeros(modulation.shape, jnp.float32)
    grad_shards = [None] * layer_count
    for layer_idx in reversed(range(layer_count)):
        back_mats = (
            lax.all_gather(s_qkv[layer_idx], ("clip", "seq"), axis=0, tiled=True),
            lax.all_gather(s_proj[layer_idx], ("clip", "seq"), axis=0, tiled=True),
            lax.all_gather(t_qkv[layer_idx], ("clip", "seq"), axis=0, tiled=True),
            lax.all_gather(t_proj[layer_idx], ("clip", "seq"), axis=0, tiled=True),
            lax.all_gather(c_query[layer_idx], ("clip", "seq"), axis=0, tiled=True),
            lax.all_gather(c_kv[layer_idx], ("clip", "seq"), axis=0, tiled=True),
            lax.all_gather(c_proj[layer_idx], ("clip", "seq"), axis=0, tiled=True),
            lax.all_gather(mlp_in[layer_idx], ("clip", "seq"), axis=0, tiled=True),
            lax.all_gather(mlp_out[layer_idx], ("clip", "seq"), axis=0, tiled=True),
            lax.all_gather(vectors[layer_idx], ("clip", "seq"), axis=1, tiled=True),
        )
        grad_hidden, layer_grads, text_part, table_part = layer_backward(
            grad_hidden, saved_list[layer_idx], back_mats, text, text_mask, heads, frame_count
        )
        grad_text = grad_text + text_part
        grad_mod = grad_mod + table_part
        grad_shards[layer_idx] = (
            lax.psum_scatter(layer_grads[0], ("clip", "seq"), scatter_dimension=0, tiled=True),
            lax.psum_scatter(layer_grads[1], ("clip", "seq"), scatter_dimension=0, tiled=True),
            lax.psum_scatter(layer_grads[2], ("clip", "seq"), scatter_dimension=0, tiled=True),
            lax.psum_scatter(layer_grads[3], ("clip", "seq"), scatter_dimension=0, tiled=True),
            lax.psum_scatter(layer_grads[4], ("clip", "seq"), scatter_dimension=0, tiled=True),
            lax.psum_scatter(layer_grads[5], ("clip", "seq"), scatter_dimension=0, tiled=True),
            lax.psum_scatter(layer_grads[6], ("clip", "seq"), scatter_dimension=0, tiled=True),
            lax.psum_scatter(layer_grads[7], ("clip", "seq"), scatter_dimension=0, tiled=True),
            lax.psum_scatter(layer_grads[8], ("clip", "seq"), scatter_dimension=0, tiled=True),
            lax.psum_scatter(layer_grads[9], ("clip", "seq"), scatter_dimension=1, tiled=True),
        )
    grad_flat = grad_mod.reshape(clip_count, 6 * model_width)
    embed_float = time_embed.astype(jnp.float32)
    time_grad = lax.psum_scatter(
        lax.dot_general(
            embed_float,
            grad_flat,
            (((0,), (0,)), ((), ())),
            precision=HIGHEST,
            preferred_element_type=jnp.float32,
        ),
        ("clip", "seq"),
        scatter_dimension=0,
        tiled=True,
    )
    text_grad = lax.psum_scatter(
        grad_text.astype(jnp.bfloat16), "seq", scatter_dimension=2, tiled=True
    ).astype(jnp.float32)
    stacked = [jnp.stack([grad_shards[0][member]]) for member in range(10)]
    return (
        output,
        grad_hidden.reshape(tokens.shape),
        text_grad,
        time_grad,
        stacked[0],
        stacked[1],
        stacked[2],
        stacked[3],
        stacked[4],
        stacked[5],
        stacked[6],
        stacked[7],
        stacked[8],
        stacked[9],
    )


ROWS = 36
PADDED = 40
HALF = 2304
ORDERS = ("xy", "yx", "xy", "yx")
SWAP = {"x": [(i, i ^ 2) for i in range(8)], "y": [(i, i ^ 4) for i in range(8)], "k": [(i, i ^ 1) for i in range(8)]}


def mesh_coords():
    clip_at = lax.axis_index("clip")
    seq_at = lax.axis_index("seq")
    return clip_at, lax.div(seq_at, 4), lax.rem(lax.div(seq_at, 2), 2), lax.rem(seq_at, 2)


def swap(arr, axis):
    return lax.ppermute(arr, "seq", SWAP[axis])


def turn(arr, d):
    return lax.ppermute(arr, "clip", [(i, (i + d) % 4) for i in range(4)])


def row_place(order, at):
    z, y, x, k = at
    spots = jnp.arange(2 * 16 * PADDED)
    row, back = spots % PADDED, (spots // PADDED) % 4
    first, second, core = (spots // (4 * PADDED)) % 2, (spots // (8 * PADDED)) % 2, spots // (16 * PADDED)
    step_x, step_y = (first, second) if order == "xy" else (second, first)
    owner = ((z + 4 - back) % 4) * 8 + (y ^ step_y) * 4 + (x ^ step_x) * 2 + (k ^ core)
    source = jnp.where(row < ROWS, owner * ROWS + row, -1)
    return (jnp.arange(32 * ROWS)[:, None] == source[None, :]).astype(jnp.bfloat16)


def gather_stage(own, order, place):
    block = own[None]
    block = jnp.concatenate([block] + [turn(block, d) for d in (1, 2, 3)], axis=0)
    for axis in order:
        block = jnp.concatenate([block, swap(block, axis)], axis=0)
    other = swap(block, "k")
    half = place.shape[1] // 2
    low = product(place[:, :half], block.reshape(half, -1))
    return (low + product(place[:, half:], other.reshape(half, -1))).astype(jnp.bfloat16)


def scatter_stage(total, order, at):
    k = at[3]
    block = total.reshape(2, 2, 2, 4, PADDED, HALF)
    block = block[:, 0] + swap(block[:, 1], order[1])
    block = block[:, 0] + swap(block[:, 1], order[0])
    kept = block[:, 0].astype(jnp.float32)
    for d in (1, 2, 3):
        kept = kept + turn(block[:, d], 4 - d).astype(jnp.float32)
    mine, other = kept[0], swap(kept[1], "k")
    low, high = jnp.where(k == 0, mine, other), jnp.where(k == 0, other, mine)
    return jnp.concatenate([low, high], axis=1)[:ROWS]


def gather_blocks(own, at):
    z, y, x, k = at
    block = jnp.stack([own] + [turn(own, d) for d in (1, 2, 3)])
    block = jnp.stack([lax.dynamic_index_in_dim(block, (z + 4 - i) % 4, 0, keepdims=False) for i in range(4)])

    def both(arr, axis, bit):
        other = swap(arr, axis)
        return jnp.stack([jnp.where(bit == 0, arr, other), jnp.where(bit == 0, other, arr)], axis=-3)

    block = both(both(both(block[:, None], "y", y)[:, 0], "x", x), "k", k)
    return block.reshape(32 * own.shape[0], own.shape[1])


def scatter_blocks(total, at):
    z, y, x, k = at
    block = total.reshape(4, 2, 2, 2, 144, 640)

    def halve(arr, axis, name, bit):
        sent = lax.dynamic_index_in_dim(arr, 1 - bit, axis, keepdims=False)
        return lax.dynamic_index_in_dim(arr, bit, axis, keepdims=False) + swap(sent, name)

    block = halve(halve(block, 2, "x", x), 1, "y", y)
    kept = lax.dynamic_index_in_dim(block, z, 0, keepdims=False).astype(jnp.float32)
    for d in (1, 2, 3):
        sent = lax.dynamic_index_in_dim(block, (z + d) % 4, 0, keepdims=False)
        kept = kept + turn(sent, d).astype(jnp.float32)
    mine = lax.dynamic_index_in_dim(kept, k, 0, keepdims=False)
    other = swap(lax.dynamic_index_in_dim(kept, 1 - k, 0, keepdims=False), "k")
    low, high = jnp.where(k == 0, mine, other), jnp.where(k == 0, other, mine)
    return jnp.concatenate([low, high[:, 128:]], axis=1)


def natural_qkv(inputs, weight, query_bias, value_bias, heads):
    width = query_bias.shape[0]
    bias_row = jnp.concatenate([query_bias, jnp.zeros_like(query_bias), value_bias])
    packed = (product(inputs, weight) + bias_row).astype(jnp.bfloat16)
    return tuple(split_heads(packed[..., i * width : (i + 1) * width], heads) for i in range(3))


def fast_device(
    tokens,
    text,
    timesteps,
    text_counts,
    out_grad,
    time_weight,
    s_qkv,
    s_proj,
    t_qkv,
    t_proj,
    c_query,
    c_kv,
    c_proj,
    mlp_in,
    mlp_out,
    vectors,
):
    heads = HEADS
    _, frame_count, patch_count, width = tokens.shape
    rows = frame_count * patch_count
    z, y, x, k = mesh_coords()
    shard = z * 8 + lax.axis_index("seq")
    pad = ((0, 4), (0, 0))
    own = [
        jnp.pad(jnp.concatenate([s_qkv[0], s_proj[0]], axis=1), pad),
        jnp.pad(jnp.concatenate([t_qkv[0], t_proj[0]], axis=1), pad),
        jnp.pad(jnp.concatenate([c_query[0], c_kv[0], c_proj[0]], axis=1), pad),
        jnp.pad(mlp_in[0], pad),
    ]
    places = [row_place(order, (z, y, x, k)) for order in ORDERS]
    stages = [gather_stage(own[i], ORDERS[i], places[i]) for i in range(4)]
    w_out = gather_blocks(mlp_out[0], (z, y, x, k))
    w_sqkv, w_sproj = stages[0][:, :3456], stages[0][:, 3456:]
    w_tqkv, w_tproj = stages[1][:, :3456], stages[1][:, 3456:]
    w_cquery, w_ckv, w_cproj = stages[2][:, :1152], stages[2][:, 1152:3456], stages[2][:, 3456:]
    w_in = stages[3]

    embed = jax.nn.silu(timestep_embed(timesteps, width)).astype(jnp.bfloat16)
    own_embed = lax.dynamic_slice_in_dim(embed, shard * ROWS, ROWS, axis=1)
    mod_part = product(own_embed, time_weight)
    own_vec = jnp.pad(vectors[0].astype(jnp.float32), ((0, 0), (0, width - ROWS)))
    own_vec = jnp.roll(own_vec, shard * ROWS, axis=1).reshape(4, 5 * width)
    spread = lax.psum(jnp.concatenate([mod_part, own_vec], axis=1), ("clip", "seq"))
    modulation = lax.dynamic_slice_in_dim(spread[:, : 6 * width], z, 1, axis=0)
    modulation = modulation.reshape(1, 6, width)
    vec_float = spread[:, 6 * width :].reshape(20, width)
    hidden = tokens.astype(jnp.float32).reshape(1, rows, width)
    out_rows = out_grad.astype(jnp.float32).reshape(1, rows, width)
    text_mask = (jnp.arange(text.shape[1])[None, :] < text_counts[:, None])[:, None, None, :]

    mod_table = modulation + vec_float[10:16][None]
    gate_one, gate_two = mod_table[:, None, 2], mod_table[:, None, 5]
    normed = modulate(hidden, mod_table[:, 0], mod_table[:, 1]).astype(jnp.bfloat16)
    frames = normed.reshape(frame_count, patch_count, width)
    s_parts = natural_qkv(frames, w_sqkv, vec_float[0], vec_float[1], heads)
    s_mixed, s_total = attend_forward(*s_parts, None, SPATIAL)
    s_flat = merge_heads(s_mixed)
    s_branch = (product(s_flat, w_sproj) + vec_float[2]).reshape(1, rows, width)
    hidden_one = hidden + gate_one * s_branch
    moved = lax.all_to_all(
        hidden_one.astype(jnp.bfloat16).reshape(1, frame_count, patch_count, width),
        "seq",
        split_axis=2,
        concat_axis=1,
        tiled=True,
    )
    t_parts = natural_qkv(moved, w_tqkv, vec_float[3], vec_float[4], heads)
    t_mixed, t_total = attend_forward(*t_parts, None, TEMPORAL)
    t_flat = merge_heads(t_mixed)
    t_branch = (product(t_flat, w_tproj) + vec_float[5]).astype(jnp.bfloat16)
    t_back = lax.all_to_all(t_branch, "seq", split_axis=1, concat_axis=2, tiled=True).reshape(1, rows, width)
    hidden_two = hidden_one + gate_one * t_back.astype(jnp.float32)
    cross_in = hidden_two.astype(jnp.bfloat16)
    c_query_rows = split_heads((product(cross_in, w_cquery) + vec_float[6]).astype(jnp.bfloat16), heads)
    kv_bias = jnp.concatenate([jnp.zeros_like(vec_float[7]), vec_float[7]])
    kv_rows = (product(text, w_ckv) + kv_bias).astype(jnp.bfloat16)
    c_key, c_value = split_heads(kv_rows[..., :width], heads), split_heads(kv_rows[..., width:], heads)
    c_mixed, c_total = attend_forward(c_query_rows, c_key, c_value, text_mask, CROSS)
    c_flat = merge_heads(c_mixed)
    hidden_three = hidden_two + (product(c_flat, w_cproj) + vec_float[8])
    normed_two = modulate(hidden_three, mod_table[:, 3], mod_table[:, 4]).astype(jnp.bfloat16)
    inner_act = product(normed_two, w_in) + vec_float[16:].reshape(-1)
    gelu_out = jax.nn.gelu(inner_act, approximate=True).astype(jnp.bfloat16)
    mlp_branch = product(gelu_out, w_out) + vec_float[9]
    hidden_four = hidden_three + gate_two * mlp_branch

    core_swap = [(i, i ^ 1) for i in range(8)]

    def pair(arr):
        flat = arr.reshape(-1, arr.shape[-1])
        return jnp.concatenate([flat, lax.ppermute(flat, "seq", core_swap)], axis=0)

    def choose(low, high):
        return jnp.where(k == 0, low, high)

    def sums_of(left, right):
        return lax.dot_general(left, right, (((0,), (0,)), ((), ())), preferred_element_type=jnp.float32).astype(
            jnp.bfloat16
        )

    def packed_rows(arr, stage):
        return product(arr, places[stage]).astype(jnp.bfloat16)

    grad_mlp = (out_rows * gate_two).astype(jnp.bfloat16)
    grad_gate_two = jnp.sum(out_rows * mlp_branch, axis=1)
    pair_mlp = pair(grad_mlp)
    sum_out = sums_of(pair(gelu_out), choose(pair_mlp[:, :640], pair_mlp[:, 512:]))
    bias_out = column_sum(grad_mlp)
    grad_gelu = product_back(grad_mlp, w_out)
    gelu_pull = jax.vjp(partial(jax.nn.gelu, approximate=True), inner_act)[1]
    grad_inner = gelu_pull(grad_gelu)[0].astype(jnp.bfloat16)
    pair_inner = pair(grad_inner)
    sum_in = sums_of(packed_rows(pair(normed_two), 3), choose(pair_inner[:, :HALF], pair_inner[:, HALF:]))
    bias_in = column_sum(grad_inner)
    norm_pull = jax.vjp(modulate, hidden_three, mod_table[:, 3], mod_table[:, 4])[1]
    grad_three, grad_shift_two, grad_scale_two = norm_pull(product_back(grad_inner, w_in))
    grad_three = out_rows + grad_three
    grad_cross = grad_three.astype(jnp.bfloat16)
    bias_cproj = column_sum(grad_cross)
    grad_cmixed = split_heads(product_back(grad_cross, w_cproj).astype(jnp.bfloat16), heads)
    cq_grad, ck_grad, cv_grad = attend_backward(
        c_query_rows, c_key, c_value, text_mask, c_total, grad_cmixed, CROSS
    )
    grad_cquery = merge_heads(cq_grad).astype(jnp.bfloat16)
    bias_cquery = column_sum(grad_cquery)
    grad_two = grad_three + product_back(grad_cquery, w_cquery)
    grad_kv = jnp.concatenate([merge_heads(ck_grad), merge_heads(cv_grad)], axis=-1).astype(jnp.bfloat16)
    bias_cvalue = column_sum(grad_kv[..., width:])
    text_part = product_back(grad_kv, w_ckv)
    pair_kv = pair(grad_kv)
    text_two = jnp.concatenate([text[0], text[0]], axis=0)
    sum_kv = sums_of(packed_rows(text_two, 2), choose(pair_kv[:, :width], pair_kv[:, width:]))
    sum_side = sums_of(packed_rows(choose(pair(cross_in), pair(c_flat)), 2), choose(pair(grad_cquery), pair(grad_cross)))
    sum_cross = choose(jnp.concatenate([sum_side, sum_kv], 1), jnp.concatenate([sum_kv, sum_side], 1))

    grad_gate_one = jnp.sum(grad_two * t_back.astype(jnp.float32), axis=1)
    grad_temporal = (grad_two * gate_one).astype(jnp.bfloat16).reshape(1, frame_count, patch_count, width)
    grad_places = lax.all_to_all(grad_temporal, "seq", split_axis=2, concat_axis=1, tiled=True)
    bias_tproj = column_sum(grad_places)
    grad_tmixed = split_heads(product_back(grad_places, w_tproj).astype(jnp.bfloat16), heads)

    def stage_sums(grads, inputs, flat, proj_grad, weight, stage):
        packed_grad = jnp.concatenate([merge_heads(part) for part in grads], axis=-1).astype(jnp.bfloat16)
        pair_grad, pair_in = pair(packed_grad), pair(inputs)
        low = sums_of(packed_rows(pair_in, stage), choose(pair_grad[:, :width], pair_grad[:, 2 * width :]))
        high = sums_of(
            packed_rows(choose(pair_in, pair(flat)), stage), choose(pair_grad[:, width : 2 * width], pair(proj_grad))
        )
        return (
            jnp.concatenate([low, high], axis=1),
            product_back(packed_grad, weight),
            column_sum(packed_grad[..., :width]),
            column_sum(packed_grad[..., 2 * width :]),
        )

    t_grads = attend_backward(*t_parts, None, t_total, grad_tmixed, TEMPORAL)
    sum_t, grad_moved, bias_tquery, bias_tvalue = stage_sums(t_grads, moved, t_flat, grad_places, w_tqkv, 1)
    grad_frames = lax.all_to_all(
        grad_moved.astype(jnp.bfloat16), "seq", split_axis=1, concat_axis=2, tiled=True
    )
    grad_one = grad_two + grad_frames.astype(jnp.float32).reshape(1, rows, width)
    grad_gate_one = grad_gate_one + jnp.sum(grad_one * s_branch, axis=1)
    grad_spatial = (grad_one * gate_one).astype(jnp.bfloat16).reshape(frame_count, patch_count, width)
    bias_sproj = column_sum(grad_spatial)
    grad_smixed = split_heads(product_back(grad_spatial, w_sproj).astype(jnp.bfloat16), heads)
    s_grads = attend_backward(*s_parts, None, s_total, grad_smixed, SPATIAL)
    sum_s, grad_normed, bias_squery, bias_svalue = stage_sums(s_grads, frames, s_flat, grad_spatial, w_sqkv, 0)
    first_pull = jax.vjp(modulate, hidden, mod_table[:, 0], mod_table[:, 1])[1]
    grad_zero, grad_shift_one, grad_scale_one = first_pull(grad_normed.reshape(1, rows, width))
    grad_input = grad_one + grad_zero

    own_s, own_t, own_c, own_in = [
        scatter_stage(total, ORDERS[i], (z, y, x, k))
        for i, total in enumerate([sum_s, sum_t, sum_cross, sum_in])
    ]
    own_out = scatter_blocks(sum_out, (z, y, x, k))

    grad_table = jnp.stack(
        [grad_shift_one, grad_scale_one, grad_gate_one, grad_shift_two, grad_scale_two, grad_gate_two], axis=1
    )[0]
    bias_rows = jnp.stack(
        [
            bias_squery,
            bias_svalue,
            bias_sproj,
            bias_tquery,
            bias_tvalue,
            bias_tproj,
            bias_cquery,
            bias_cvalue,
            bias_cproj,
            bias_out,
        ]
    )
    small = jnp.concatenate([bias_rows, grad_table, bias_in.reshape(4, width)], axis=0)
    own_clip = (jnp.arange(4) == z).astype(jnp.float32)[:, None, None]
    small = lax.psum(own_clip * small[None], ("clip", "seq"))
    vec_grad = lax.dynamic_slice_in_dim(jnp.sum(small, axis=0), shard * ROWS, ROWS, axis=1)
    time_grad = lax.dot_general(
        own_embed.astype(jnp.float32),
        small[:, 10:16].reshape(4, 6 * width),
        (((0,), (0,)), ((), ())),
        precision=HIGHEST,
        preferred_element_type=jnp.float32,
    )
    text_grad = lax.psum_scatter(text_part, "seq", scatter_dimension=2, tiled=True)
    return (
        hidden_four.reshape(tokens.shape),
        grad_input.reshape(tokens.shape),
        text_grad,
        time_grad,
        own_s[None, :, :3456],
        own_s[None, :, 3456:],
        own_t[None, :, :3456],
        own_t[None, :, 3456:],
        own_c[None, :, :1152],
        own_c[None, :, 1152:3456],
        own_c[None, :, 3456:],
        own_in[None],
        own_out[None],
        vec_grad[None],
    )


def run_device(sizes, tokens, *rest):
    fits = (sizes["clip"], sizes["seq"]) == (4, 8) and tokens.shape == (1, 2, 256, 1152)
    return (fast_device if fits else per_device)(tokens, *rest)


def solution(mesh):
    placed = (
        P("clip", "seq", None, None),
        P("clip", None, None),
        P(),
        P("clip"),
        P("clip", "seq", None, None),
        P(("clip", "seq"), None),
        P(None, ("clip", "seq"), None),
        P(None, ("clip", "seq"), None),
        P(None, ("clip", "seq"), None),
        P(None, ("clip", "seq"), None),
        P(None, ("clip", "seq"), None),
        P(None, ("clip", "seq"), None),
        P(None, ("clip", "seq"), None),
        P(None, ("clip", "seq"), None),
        P(None, ("clip", "seq"), None),
        P(None, None, ("clip", "seq")),
    )
    return jax.shard_map(
        partial(run_device, dict(mesh.shape)),
        mesh=mesh,
        in_specs=placed,
        out_specs=(
            P("clip", "seq", None, None),
            P("clip", "seq", None, None),
            P("clip", None, "seq"),
            P(("clip", "seq"), None),
            P(None, ("clip", "seq"), None),
            P(None, ("clip", "seq"), None),
            P(None, ("clip", "seq"), None),
            P(None, ("clip", "seq"), None),
            P(None, ("clip", "seq"), None),
            P(None, ("clip", "seq"), None),
            P(None, ("clip", "seq"), None),
            P(None, ("clip", "seq"), None),
            P(None, ("clip", "seq"), None),
            P(None, None, ("clip", "seq")),
        ),
        check_vma=False,
    )
```

```python
from functools import partial
import math

import jax
import jax.numpy as jnp
from jax import lax
from jax.sharding import PartitionSpec as P

HEADS = 16


EPSILON = 1e-06
HIGHEST = lax.Precision.HIGHEST
SPATIAL = ("bqhe", "bkhe", "bhqk")
TEMPORAL = ("cqphe", "ckphe", "cphqk")
CROSS = ("cqhe", "ckhe", "chqk")


def product(left_arr, right_arr):
    return lax.dot_general(
        left_arr,
        right_arr,
        (((left_arr.ndim - 1,), (0,)), ((), ())),
        preferred_element_type=jnp.float32,
    )


def product_back(grad_arr, weight):
    return lax.dot_general(
        grad_arr,
        weight,
        (((grad_arr.ndim - 1,), (1,)), ((), ())),
        preferred_element_type=jnp.float32,
    )


def outer_sum(left_arr, right_arr):
    left_rows = left_arr.reshape(-1, left_arr.shape[-1])
    right_rows = right_arr.reshape(-1, right_arr.shape[-1])
    return lax.dot_general(
        left_rows, right_rows, (((0,), (0,)), ((), ())), preferred_element_type=jnp.float32
    )


def column_sum(grad_arr):
    return jnp.sum(grad_arr.astype(jnp.float32).reshape(-1, grad_arr.shape[-1]), axis=0)


def timestep_embed(step_values, model_width):
    half_width = model_width // 2
    frequency = jnp.exp(-math.log(10000.0) * jnp.arange(half_width, dtype=jnp.float32) / half_width)
    angles = step_values.astype(jnp.float32)[:, None] * frequency[None, :]
    return jnp.concatenate([jnp.cos(angles), jnp.sin(angles)], axis=-1)


def modulate(hidden, shift_row, scale_row):
    centered = hidden - jnp.mean(hidden, axis=-1, keepdims=True)
    normed = centered * lax.rsqrt(jnp.mean(centered * centered, axis=-1, keepdims=True) + EPSILON)
    return normed * (1.0 + scale_row[:, None, :]) + shift_row[:, None, :]


def split_heads(packed_arr, heads):
    return packed_arr.reshape(packed_arr.shape[:-1] + (heads, packed_arr.shape[-1] // heads))


def merge_heads(head_arr):
    return head_arr.reshape(head_arr.shape[:-2] + (head_arr.shape[-2] * head_arr.shape[-1],))


def attend_scores(queries, key_rows, key_mask, forms):
    query_form, key_form, score_form = forms
    scale_factor = queries.shape[-1] ** (-0.5)
    scores = (
        jnp.einsum(
            query_form + "," + key_form + "->" + score_form,
            queries,
            key_rows,
            preferred_element_type=jnp.float32,
        )
        * scale_factor
    )
    if key_mask is not None:
        scores = jnp.where(key_mask, scores, -1000000000.0)
    return scores


def attend_forward(queries, key_rows, values, key_mask, forms):
    query_form, key_form, score_form = forms
    scores = attend_scores(queries, key_rows, key_mask, forms)
    top_score = jnp.max(scores, axis=-1, keepdims=True)
    log_total = top_score + jnp.log(jnp.sum(jnp.exp(scores - top_score), axis=-1, keepdims=True))
    attn_probs = jnp.exp(scores - log_total).astype(jnp.bfloat16)
    mixed_heads = jnp.einsum(
        score_form + "," + key_form + "->" + query_form,
        attn_probs,
        values,
        preferred_element_type=jnp.float32,
    )
    return (mixed_heads.astype(jnp.bfloat16), log_total)


def attend_backward(queries, key_rows, values, key_mask, log_total, grad_mixed, forms):
    query_form, key_form, score_form = forms
    scale_factor = queries.shape[-1] ** (-0.5)
    scores = attend_scores(queries, key_rows, key_mask, forms)
    attn_probs = jnp.exp(scores - log_total)
    grad_probs = jnp.einsum(
        query_form + "," + key_form + "->" + score_form,
        grad_mixed,
        values,
        preferred_element_type=jnp.float32,
    )
    inner_dot = jnp.sum(attn_probs * grad_probs, axis=-1, keepdims=True)
    grad_scores = (attn_probs * (grad_probs - inner_dot)).astype(jnp.bfloat16)
    grad_values = jnp.einsum(
        score_form + "," + query_form + "->" + key_form,
        attn_probs.astype(jnp.bfloat16),
        grad_mixed,
        preferred_element_type=jnp.float32,
    )
    grad_queries = (
        jnp.einsum(
            score_form + "," + key_form + "->" + query_form,
            grad_scores,
            key_rows,
            preferred_element_type=jnp.float32,
        )
        * scale_factor
    )
    grad_keys = (
        jnp.einsum(
            score_form + "," + query_form + "->" + key_form,
            grad_scores,
            queries,
            preferred_element_type=jnp.float32,
        )
        * scale_factor
    )
    return (grad_queries, grad_keys, grad_values)


def project_qkv(inputs, weight, query_bias, value_bias, heads):
    model_width = query_bias.shape[0]
    bias_row = jnp.concatenate([query_bias, jnp.zeros_like(query_bias), value_bias]).astype(
        jnp.float32
    )
    packed = (product(inputs, weight) + bias_row).astype(jnp.bfloat16)
    return (
        split_heads(packed[..., :model_width], heads),
        split_heads(packed[..., model_width : 2 * model_width], heads),
        split_heads(packed[..., 2 * model_width :], heads),
    )


def qkv_backward(grad_parts, inputs, weight):
    model_width = weight.shape[0]
    packed_grad = jnp.concatenate(
        [merge_heads(grad_part) for grad_part in grad_parts], axis=-1
    ).astype(jnp.bfloat16)
    return (
        outer_sum(inputs, packed_grad),
        product_back(packed_grad, weight),
        column_sum(packed_grad[..., :model_width]),
        column_sum(packed_grad[..., 2 * model_width :]),
    )


def layer_forward(hidden, layer_mats, modulation, text, text_mask, heads, frame_count):
    w_sqkv, w_sproj, w_tqkv, w_tproj, w_cquery, w_ckv, w_cproj, w_in, w_out, vec_rows = layer_mats
    clip_count, row_count, model_width = hidden.shape
    patch_count = row_count // frame_count
    vec_float = vec_rows.astype(jnp.float32)
    mod_table = modulation + vec_float[10:16][None]
    gate_one = mod_table[:, None, 2]
    normed = (
        modulate(hidden, mod_table[:, 0], mod_table[:, 1])
        .astype(jnp.bfloat16)
        .reshape(clip_count * frame_count, patch_count, model_width)
    )
    s_query, s_key, s_value = project_qkv(normed, w_sqkv, vec_rows[0], vec_rows[1], heads)
    s_mixed, s_total = attend_forward(s_query, s_key, s_value, None, SPATIAL)
    s_flat = merge_heads(s_mixed)
    s_branch = (product(s_flat, w_sproj) + vec_float[2]).reshape(clip_count, row_count, model_width)
    hidden_one = hidden + gate_one * s_branch
    frames_view = hidden_one.astype(jnp.bfloat16).reshape(
        clip_count, frame_count, patch_count, model_width
    )
    moved = lax.all_to_all(frames_view, "seq", split_axis=2, concat_axis=1, tiled=True)
    t_query, t_key, t_value = project_qkv(moved, w_tqkv, vec_rows[3], vec_rows[4], heads)
    t_mixed, t_total = attend_forward(t_query, t_key, t_value, None, TEMPORAL)
    t_flat = merge_heads(t_mixed)
    t_branch = (product(t_flat, w_tproj) + vec_float[5]).astype(jnp.bfloat16)
    t_back = lax.all_to_all(t_branch, "seq", split_axis=1, concat_axis=2, tiled=True).reshape(
        clip_count, row_count, model_width
    )
    hidden_two = hidden_one + gate_one * t_back.astype(jnp.float32)
    cross_in = hidden_two.astype(jnp.bfloat16)
    c_query = split_heads((product(cross_in, w_cquery) + vec_float[6]).astype(jnp.bfloat16), heads)
    kv_bias = jnp.concatenate([jnp.zeros_like(vec_float[7]), vec_float[7]])
    c_packed = (product(text, w_ckv) + kv_bias).astype(jnp.bfloat16)
    c_key = split_heads(c_packed[..., :model_width], heads)
    c_value = split_heads(c_packed[..., model_width:], heads)
    c_mixed, c_total = attend_forward(c_query, c_key, c_value, text_mask, CROSS)
    c_flat = merge_heads(c_mixed)
    hidden_three = hidden_two + (product(c_flat, w_cproj) + vec_float[8])
    normed_two = modulate(hidden_three, mod_table[:, 3], mod_table[:, 4]).astype(jnp.bfloat16)
    inner_act = product(normed_two, w_in) + vec_float[16:].reshape(-1)
    gelu_out = jax.nn.gelu(inner_act, approximate=True).astype(jnp.bfloat16)
    mlp_branch = product(gelu_out, w_out) + vec_float[9]
    hidden_four = hidden_three + mod_table[:, None, 5] * mlp_branch
    saved = dict(
        mod_table=mod_table,
        hidden=hidden,
        normed=normed,
        s_query=s_query,
        s_key=s_key,
        s_value=s_value,
        s_total=s_total,
        s_flat=s_flat,
        s_branch=s_branch,
        moved=moved,
        t_query=t_query,
        t_key=t_key,
        t_value=t_value,
        t_total=t_total,
        t_flat=t_flat,
        t_back=t_back,
        cross_in=cross_in,
        c_query=c_query,
        c_key=c_key,
        c_value=c_value,
        c_total=c_total,
        c_flat=c_flat,
        hidden_three=hidden_three,
        normed_two=normed_two,
        inner_act=inner_act,
        gelu_out=gelu_out,
        mlp_branch=mlp_branch,
    )
    return (hidden_four, saved)


def layer_backward(grad_hidden, saved, layer_mats, text, text_mask, heads, frame_count):
    w_sqkv, w_sproj, w_tqkv, w_tproj, w_cquery, w_ckv, w_cproj, w_in, w_out, vec_rows = layer_mats
    clip_count, row_count, model_width = grad_hidden.shape
    patch_count = row_count // frame_count
    mod_table = saved["mod_table"]
    gate_one = mod_table[:, None, 2]
    gate_two = mod_table[:, None, 5]
    grad_mlp = (grad_hidden * gate_two).astype(jnp.bfloat16)
    grad_gate_two = jnp.sum(grad_hidden * saved["mlp_branch"], axis=1)
    grad_w_out = outer_sum(saved["gelu_out"], grad_mlp)
    bias_out = column_sum(grad_mlp)
    grad_gelu = product_back(grad_mlp, w_out)
    gelu_pull = jax.vjp(partial(jax.nn.gelu, approximate=True), saved["inner_act"])[1]
    grad_inner = gelu_pull(grad_gelu)[0].astype(jnp.bfloat16)
    grad_w_in = outer_sum(saved["normed_two"], grad_inner)
    bias_in = column_sum(grad_inner)
    grad_normed_two = product_back(grad_inner, w_in)
    norm_pull = jax.vjp(modulate, saved["hidden_three"], mod_table[:, 3], mod_table[:, 4])[1]
    grad_three, grad_shift_two, grad_scale_two = norm_pull(grad_normed_two)
    grad_three = grad_hidden + grad_three
    grad_cross = grad_three.astype(jnp.bfloat16)
    grad_w_cproj = outer_sum(saved["c_flat"], grad_cross)
    bias_cproj = column_sum(grad_cross)
    grad_cmixed = split_heads(product_back(grad_cross, w_cproj).astype(jnp.bfloat16), heads)
    cq_grad, ck_grad, cv_grad = attend_backward(
        saved["c_query"],
        saved["c_key"],
        saved["c_value"],
        text_mask,
        saved["c_total"],
        grad_cmixed,
        CROSS,
    )
    grad_cquery = merge_heads(cq_grad).astype(jnp.bfloat16)
    grad_w_cquery = outer_sum(saved["cross_in"], grad_cquery)
    bias_cquery = column_sum(grad_cquery)
    grad_two = grad_three + product_back(grad_cquery, w_cquery)
    grad_kv = jnp.concatenate([merge_heads(ck_grad), merge_heads(cv_grad)], axis=-1).astype(
        jnp.bfloat16
    )
    grad_w_ckv = outer_sum(text, grad_kv)
    bias_cvalue = column_sum(grad_kv[..., model_width:])
    text_part = product_back(grad_kv, w_ckv)
    grad_gate_one = jnp.sum(grad_two * saved["t_back"].astype(jnp.float32), axis=1)
    grad_temporal = (
        (grad_two * gate_one)
        .astype(jnp.bfloat16)
        .reshape(clip_count, frame_count, patch_count, model_width)
    )
    grad_places = lax.all_to_all(grad_temporal, "seq", split_axis=2, concat_axis=1, tiled=True)
    grad_w_tproj = outer_sum(saved["t_flat"], grad_places)
    bias_tproj = column_sum(grad_places)
    grad_tmixed = split_heads(product_back(grad_places, w_tproj).astype(jnp.bfloat16), heads)
    temporal_grads = attend_backward(
        saved["t_query"],
        saved["t_key"],
        saved["t_value"],
        None,
        saved["t_total"],
        grad_tmixed,
        TEMPORAL,
    )
    grad_w_tqkv, grad_moved, bias_tquery, bias_tvalue = qkv_backward(
        temporal_grads, saved["moved"], w_tqkv
    )
    grad_frames = lax.all_to_all(
        grad_moved.astype(jnp.bfloat16), "seq", split_axis=1, concat_axis=2, tiled=True
    )
    grad_one = grad_two + grad_frames.astype(jnp.float32).reshape(
        clip_count, row_count, model_width
    )
    grad_gate_one = grad_gate_one + jnp.sum(grad_one * saved["s_branch"], axis=1)
    grad_spatial = (
        (grad_one * gate_one)
        .astype(jnp.bfloat16)
        .reshape(clip_count * frame_count, patch_count, model_width)
    )
    grad_w_sproj = outer_sum(saved["s_flat"], grad_spatial)
    bias_sproj = column_sum(grad_spatial)
    grad_smixed = split_heads(product_back(grad_spatial, w_sproj).astype(jnp.bfloat16), heads)
    spatial_grads = attend_backward(
        saved["s_query"],
        saved["s_key"],
        saved["s_value"],
        None,
        saved["s_total"],
        grad_smixed,
        SPATIAL,
    )
    grad_w_sqkv, grad_normed, bias_squery, bias_svalue = qkv_backward(
        spatial_grads, saved["normed"], w_sqkv
    )
    first_pull = jax.vjp(modulate, saved["hidden"], mod_table[:, 0], mod_table[:, 1])[1]
    grad_zero, grad_shift_one, grad_scale_one = first_pull(
        grad_normed.reshape(clip_count, row_count, model_width)
    )
    grad_input = grad_one + grad_zero
    grad_table = jnp.stack(
        [
            grad_shift_one,
            grad_scale_one,
            grad_gate_one,
            grad_shift_two,
            grad_scale_two,
            grad_gate_two,
        ],
        axis=1,
    )
    bias_rows = jnp.stack(
        [
            bias_squery,
            bias_svalue,
            bias_sproj,
            bias_tquery,
            bias_tvalue,
            bias_tproj,
            bias_cquery,
            bias_cvalue,
            bias_cproj,
            bias_out,
        ]
    )
    vec_grad = jnp.concatenate(
        [bias_rows, jnp.sum(grad_table, axis=0), bias_in.reshape(-1, model_width)], axis=0
    )
    layer_grads = (
        grad_w_sqkv,
        grad_w_sproj,
        grad_w_tqkv,
        grad_w_tproj,
        grad_w_cquery,
        grad_w_ckv,
        grad_w_cproj,
        grad_w_in,
        grad_w_out,
        vec_grad,
    )
    return (grad_input, layer_grads, text_part, grad_table)


def per_device(
    tokens,
    text,
    timesteps,
    text_counts,
    out_grad,
    time_weight,
    s_qkv,
    s_proj,
    t_qkv,
    t_proj,
    c_query,
    c_kv,
    c_proj,
    mlp_in,
    mlp_out,
    vectors,
):
    clip_count, frame_count, patch_count, model_width = tokens.shape
    layer_count = s_qkv.shape[0]
    heads = HEADS
    clip_first = lax.axis_index("clip") * clip_count
    my_steps = lax.dynamic_slice_in_dim(timesteps, clip_first, clip_count)
    time_embed = jax.nn.silu(timestep_embed(my_steps, model_width)).astype(jnp.bfloat16)
    time_full = lax.all_gather(time_weight, ("clip", "seq"), axis=0, tiled=True)
    modulation = product(time_embed, time_full).reshape(clip_count, 6, model_width)
    text_mask = (jnp.arange(text.shape[1])[None, :] < text_counts[:, None])[:, None, None, :]
    hidden = tokens.astype(jnp.float32).reshape(clip_count, frame_count * patch_count, model_width)
    layer_mats = None
    layer_idx = 0
    layer_mats = (
        lax.all_gather(s_qkv[layer_idx], ("clip", "seq"), axis=0, tiled=True),
        lax.all_gather(s_proj[layer_idx], ("clip", "seq"), axis=0, tiled=True),
        lax.all_gather(t_qkv[layer_idx], ("clip", "seq"), axis=0, tiled=True),
        lax.all_gather(t_proj[layer_idx], ("clip", "seq"), axis=0, tiled=True),
        lax.all_gather(c_query[layer_idx], ("clip", "seq"), axis=0, tiled=True),
        lax.all_gather(c_kv[layer_idx], ("clip", "seq"), axis=0, tiled=True),
        lax.all_gather(c_proj[layer_idx], ("clip", "seq"), axis=0, tiled=True),
        lax.all_gather(mlp_in[layer_idx], ("clip", "seq"), axis=0, tiled=True),
        lax.all_gather(mlp_out[layer_idx], ("clip", "seq"), axis=0, tiled=True),
        lax.all_gather(vectors[layer_idx], ("clip", "seq"), axis=1, tiled=True),
    )
    hidden, saved = layer_forward(
        hidden, layer_mats, modulation, text, text_mask, heads, frame_count
    )
    saved_list = [saved]
    output = hidden.reshape(tokens.shape)
    grad_hidden = out_grad.astype(jnp.float32).reshape(hidden.shape)
    grad_text = jnp.zeros(text.shape, jnp.float32)
    grad_mod = jnp.zeros(modulation.shape, jnp.float32)
    grad_shards = [None] * layer_count
    for layer_idx in reversed(range(layer_count)):
        back_mats = (
            lax.all_gather(s_qkv[layer_idx], ("clip", "seq"), axis=0, tiled=True),
            lax.all_gather(s_proj[layer_idx], ("clip", "seq"), axis=0, tiled=True),
            lax.all_gather(t_qkv[layer_idx], ("clip", "seq"), axis=0, tiled=True),
            lax.all_gather(t_proj[layer_idx], ("clip", "seq"), axis=0, tiled=True),
            lax.all_gather(c_query[layer_idx], ("clip", "seq"), axis=0, tiled=True),
            lax.all_gather(c_kv[layer_idx], ("clip", "seq"), axis=0, tiled=True),
            lax.all_gather(c_proj[layer_idx], ("clip", "seq"), axis=0, tiled=True),
            lax.all_gather(mlp_in[layer_idx], ("clip", "seq"), axis=0, tiled=True),
            lax.all_gather(mlp_out[layer_idx], ("clip", "seq"), axis=0, tiled=True),
            lax.all_gather(vectors[layer_idx], ("clip", "seq"), axis=1, tiled=True),
        )
        grad_hidden, layer_grads, text_part, table_part = layer_backward(
            grad_hidden, saved_list[layer_idx], back_mats, text, text_mask, heads, frame_count
        )
        grad_text = grad_text + text_part
        grad_mod = grad_mod + table_part
        grad_shards[layer_idx] = (
            lax.psum_scatter(layer_grads[0], ("clip", "seq"), scatter_dimension=0, tiled=True),
            lax.psum_scatter(layer_grads[1], ("clip", "seq"), scatter_dimension=0, tiled=True),
            lax.psum_scatter(layer_grads[2], ("clip", "seq"), scatter_dimension=0, tiled=True),
            lax.psum_scatter(layer_grads[3], ("clip", "seq"), scatter_dimension=0, tiled=True),
            lax.psum_scatter(layer_grads[4], ("clip", "seq"), scatter_dimension=0, tiled=True),
            lax.psum_scatter(layer_grads[5], ("clip", "seq"), scatter_dimension=0, tiled=True),
            lax.psum_scatter(layer_grads[6], ("clip", "seq"), scatter_dimension=0, tiled=True),
            lax.psum_scatter(layer_grads[7], ("clip", "seq"), scatter_dimension=0, tiled=True),
            lax.psum_scatter(layer_grads[8], ("clip", "seq"), scatter_dimension=0, tiled=True),
            lax.psum_scatter(layer_grads[9], ("clip", "seq"), scatter_dimension=1, tiled=True),
        )
    grad_flat = grad_mod.reshape(clip_count, 6 * model_width)
    embed_float = time_embed.astype(jnp.float32)
    time_grad = lax.psum_scatter(
        lax.dot_general(
            embed_float,
            grad_flat,
            (((0,), (0,)), ((), ())),
            precision=HIGHEST,
            preferred_element_type=jnp.float32,
        ),
        ("clip", "seq"),
        scatter_dimension=0,
        tiled=True,
    )
    text_grad = lax.psum_scatter(
        grad_text.astype(jnp.bfloat16), "seq", scatter_dimension=2, tiled=True
    ).astype(jnp.float32)
    stacked = [jnp.stack([grad_shards[0][member]]) for member in range(10)]
    return (
        output,
        grad_hidden.reshape(tokens.shape),
        text_grad,
        time_grad,
        stacked[0],
        stacked[1],
        stacked[2],
        stacked[3],
        stacked[4],
        stacked[5],
        stacked[6],
        stacked[7],
        stacked[8],
        stacked[9],
    )


ROWS = 36
PADDED = 40
HALF = 2304
SWAP = {"x": [(i, i ^ 2) for i in range(8)], "y": [(i, i ^ 4) for i in range(8)], "k": [(i, i ^ 1) for i in range(8)]}


def mesh_coords():
    clip_at = lax.axis_index("clip")
    seq_at = lax.axis_index("seq")
    return clip_at, lax.div(seq_at, 4), lax.rem(lax.div(seq_at, 2), 2), lax.rem(seq_at, 2)


def swap(arr, axis):
    return lax.ppermute(arr, "seq", SWAP[axis])


def turn(arr, d):
    return lax.ppermute(arr, "clip", [(i, (i + d) % 4) for i in range(4)])


class Task:
    def __init__(self, steps, state):
        self.steps, self.state, self.at, self.left = steps, state, 0, 0

    def done(self):
        return self.at == len(self.steps) and not self.left

    def crosses_plane(self):
        return any(step[0] == "plane" for step in self.steps[self.at :])


class Mover:
    def __init__(self):
        self.tasks = []

    def add(self, steps, state):
        self.tasks.append(Task(steps, state))
        return self.tasks[-1]

    def tick(self, values=()):
        arrived = []
        for task in self.tasks:
            task.left = max(task.left - 1, 0)
            if task.at and not task.left and not task.tied:
                arrived.append(task)
        values, states = lax.optimization_barrier((values, [task.state for task in arrived]))
        for task, state in zip(arrived, states):
            task.state, task.tied = state, True
        busy, turning = False, False
        for task in self.tasks:
            if task.at < len(task.steps) and not task.left:
                kind, ticks, step = task.steps[task.at]
                if not (kind == "plane" and busy or kind == "z" and turning):
                    task.state = step(task.state)
                    task.at, task.left, task.tied = task.at + 1, ticks, False
            kind = task.steps[task.at - 1][0] if task.left else ""
            turning = turning or kind == "z"
            busy = busy or kind == "plane" or task.crosses_plane()
        return values

    def finish(self, task):
        while not task.done():
            self.tick()

    def drain(self):
        for task in self.tasks:
            self.finish(task)


def row_place(at):
    z, y, x, k = at
    spots = jnp.arange(32 * PADDED)
    row, back = spots % PADDED, (spots // PADDED) % 4
    step_x, step_y, core = (spots // (4 * PADDED)) % 2, (spots // (8 * PADDED)) % 2, spots // (16 * PADDED)
    owner = ((z + 4 - back) % 4) * 8 + (y ^ step_y) * 4 + (x ^ step_x) * 2 + (k ^ core)
    source = jnp.where(row < ROWS, owner * ROWS + row, -1)
    return (jnp.arange(32 * ROWS)[:, None] == source[None, :]).astype(jnp.bfloat16)


def along_z(own):
    return jnp.concatenate([own] + [turn(own, d) for d in (1, 2, 3)], axis=0)


def gather_steps():
    def start(own):
        parts = [own] + [turn(own, d) for d in (1, 2, 3)]
        return tuple(
            jnp.concatenate([part[..., i : i + HALF] for part in parts], axis=0) for i in (0, HALF)
        )

    def first(state):
        low, high = state
        return jnp.concatenate([low, swap(low, "x")], axis=0), high, swap(high, "y")

    def second(state):
        low, high, beside = state
        across = swap(jnp.concatenate([high, beside], axis=0), "x")
        return (
            jnp.concatenate([low, swap(low, "y")], axis=0),
            jnp.concatenate([high, across[:4], beside, across[4:]], axis=0),
        )

    def third(state):
        low, high = (part.reshape(16 * PADDED, HALF) for part in state)
        return (low, swap(low, "k")), (high, swap(high, "k"))

    return [("z", 1, start), ("plane", 1, first), ("plane", 2, second), ("core", 1, third)]


def gather_out_steps(at):
    z, y, x, k = at

    def both(arr, axis, bit, dim):
        other = swap(arr, axis)
        return jnp.concatenate([jnp.where(bit == 0, arr, other), jnp.where(bit == 0, other, arr)], axis=dim)

    def start(own):
        block = along_z(own[None])
        return jnp.concatenate(
            [lax.dynamic_index_in_dim(block, (z + 4 - i) % 4, 0) for i in range(4)], axis=0
        ).reshape(4, 1, 1, 1, 144, 1152)

    def first(block):
        return both(block[..., :72, :], "x", x, 2), both(block[..., 72:, :], "y", y, 1)

    def second(state):
        return both(state[0], "y", y, 1), both(state[1], "x", x, 2)

    def third(state):
        low, high = (both(part, "k", k, 3) for part in state)
        return jnp.concatenate([low, high], axis=4).reshape(32 * 144, 1152)

    return [("z", 1, start), ("plane", 1, first), ("plane", 2, second), ("core", 1, third)]


def to_owner(kept, sent, k):
    other = swap(sent, "k")
    return jnp.where(k == 0, kept, other), jnp.where(k == 0, other, kept)


def scatter_steps(k):
    def first(state):
        low, high = (part.reshape(2, 2, 2, 4, PADDED, HALF // 2) for part in state)
        return low[:, 0] + swap(low[:, 1], "y"), high[:, :, 0] + swap(high[:, :, 1], "x")

    def second(state):
        low, high = state
        return jnp.concatenate(
            [low[:, 0] + swap(low[:, 1], "x"), high[:, 0] + swap(high[:, 1], "y")], axis=-1
        )

    def third(block):
        kept = block[:, 0].astype(jnp.float32)
        for d in (1, 2, 3):
            kept = kept + turn(block[:, d], 4 - d).astype(jnp.float32)
        return kept

    def fourth(kept):
        return jnp.concatenate(to_owner(kept[0], kept[1], k), axis=1)[:ROWS]

    return [("plane", 2, first), ("plane", 1, second), ("z", 2, third), ("core", 1, fourth)]


def scatter_out_steps(at):
    z, y, x, k = at

    def halve(arr, axis, name, bit):
        sent = lax.dynamic_index_in_dim(arr, 1 - bit, axis, keepdims=False)
        return lax.dynamic_index_in_dim(arr, bit, axis, keepdims=False) + swap(sent, name)

    def first(total):
        block = total.reshape(4, 2, 2, 2, 144, 640)
        return halve(block[..., :384], 1, "y", y), halve(block[..., 384:], 2, "x", x)

    def second(state):
        return jnp.concatenate([halve(state[0], 1, "x", x), halve(state[1], 1, "y", y)], axis=-1)

    def third(block):
        kept = lax.dynamic_index_in_dim(block, z, 0, keepdims=False).astype(jnp.float32)
        for d in (1, 2, 3):
            sent = lax.dynamic_index_in_dim(block, (z + d) % 4, 0, keepdims=False)
            kept = kept + turn(sent, d).astype(jnp.float32)
        return kept

    def fourth(kept):
        mine = lax.dynamic_index_in_dim(kept, k, 0, keepdims=False)
        low, high = to_owner(mine, lax.dynamic_index_in_dim(kept, 1 - k, 0, keepdims=False), k)
        return jnp.concatenate([low, high[:, 128:]], axis=1)

    return [("plane", 2, first), ("plane", 1, second), ("z", 2, third), ("core", 1, fourth)]


def sum_over_plane(arr):
    for axis in ("k", "x", "y"):
        arr = arr + swap(arr, axis)
    return arr


def packed_product(packed, weight):
    half = packed.shape[-1] // 2
    return product(packed[..., :half], weight[0]) + product(packed[..., half:], weight[1])


def packed_back(grad_arr, weight):
    return jnp.concatenate([product_back(grad_arr, part) for part in weight], axis=-1)


def columns(weight, first, count):
    return tuple(part[:, first : first + count] for part in weight)


def fast_device(
    tokens,
    text,
    timesteps,
    text_counts,
    out_grad,
    time_weight,
    s_qkv,
    s_proj,
    t_qkv,
    t_proj,
    c_query,
    c_kv,
    c_proj,
    mlp_in,
    mlp_out,
    vectors,
):
    heads = HEADS
    _, frame_count, patch_count, width = tokens.shape
    rows = frame_count * patch_count
    at = mesh_coords()
    z, y, x, k = at
    shard = z * 8 + lax.axis_index("seq")
    place = row_place(at)

    def packed(arr):
        return product(arr, place).astype(jnp.bfloat16)

    def unpacked(arr):
        return lax.dot_general(
            arr,
            place,
            (((arr.ndim - 1,), (1,)), ((), ())),
            preferred_element_type=jnp.float32,
        ).astype(jnp.bfloat16)

    def unpacked_float(arr):
        return lax.dot_general(
            arr,
            place.astype(jnp.float32),
            (((arr.ndim - 1,), (1,)), ((), ())),
            precision=HIGHEST,
            preferred_element_type=jnp.float32,
        )

    def shard_of(*weights):
        return jnp.pad(jnp.concatenate([w[0] for w in weights], axis=1), ((0, PADDED - ROWS), (0, 0)))[None]

    mover = Mover()
    s_task = mover.add(gather_steps(), shard_of(s_qkv, s_proj))
    t_task = mover.add(gather_steps(), shard_of(t_qkv, t_proj))
    c_task = mover.add(gather_steps(), shard_of(c_query, c_kv, c_proj))
    i_task = mover.add(gather_steps(), shard_of(mlp_in))
    o_task = mover.add(gather_out_steps(at), mlp_out[0])

    embed = jax.nn.silu(timestep_embed(timesteps, width)).astype(jnp.bfloat16)
    own_embed = lax.dynamic_slice_in_dim(embed, shard * ROWS, ROWS, axis=1)
    mod_part = product(own_embed, time_weight)
    own_vec = jnp.pad(vectors[0].astype(jnp.float32), ((0, 0), (0, width - ROWS)))
    own_vec = jnp.roll(own_vec, shard * ROWS, axis=1)
    own_vec = own_vec.reshape(20, width)
    mod_part = mod_part.reshape(4, 6, width)

    def small_part(d):
        return jnp.concatenate([lax.dynamic_index_in_dim(mod_part, (z + d) % 4, 0, keepdims=False), own_vec])

    spread = small_part(0)
    for d in (1, 2, 3):
        spread = spread + turn(small_part(d), d)
    spread = sum_over_plane(spread)
    modulation, vec_float = spread[None, :6], spread[6:]
    hidden = tokens.astype(jnp.float32).reshape(1, rows, width)
    out_rows = out_grad.astype(jnp.float32).reshape(1, rows, width)
    text_mask = (jnp.arange(text.shape[1])[None, :] < text_counts[:, None])[:, None, None, :]

    def split_qkv(inputs_packed, task, query_bias, value_bias):
        low, high = task.state
        first = packed_product(inputs_packed, low)
        value = packed_product(inputs_packed, columns(high, 0, width)) + value_bias
        parts = (first[..., :width] + query_bias, first[..., width:], value)
        return tuple(split_heads(part.astype(jnp.bfloat16), heads) for part in parts)

    mod_table = modulation + vec_float[10:16][None]
    gate_one, gate_two = mod_table[:, None, 2], mod_table[:, None, 5]
    mover.finish(s_task)
    normed = modulate(hidden, mod_table[:, 0], mod_table[:, 1]).astype(jnp.bfloat16)
    frames = packed(normed.reshape(frame_count, patch_count, width))
    frames = mover.tick(frames)
    s_parts = mover.tick(split_qkv(frames, s_task, vec_float[0], vec_float[1]))
    s_mixed, s_total = attend_forward(*s_parts, None, SPATIAL)
    s_flat = mover.tick(packed(merge_heads(s_mixed)))
    s_high = columns(s_task.state[1], width, width)
    s_branch = (packed_product(s_flat, s_high) + vec_float[2]).reshape(1, rows, width)
    hidden_one = hidden + gate_one * s_branch
    moved = lax.all_to_all(
        hidden_one.astype(jnp.bfloat16).reshape(1, frame_count, patch_count, width),
        "seq",
        split_axis=2,
        concat_axis=1,
        tiled=True,
    )
    moved = mover.tick(packed(moved))
    mover.finish(t_task)
    t_parts = mover.tick(split_qkv(moved, t_task, vec_float[3], vec_float[4]))
    t_mixed, t_total = attend_forward(*t_parts, None, TEMPORAL)
    t_flat = mover.tick(packed(merge_heads(t_mixed)))
    t_high = columns(t_task.state[1], width, width)
    t_branch = (packed_product(t_flat, t_high) + vec_float[5]).astype(jnp.bfloat16)
    t_back = lax.all_to_all(t_branch, "seq", split_axis=1, concat_axis=2, tiled=True).reshape(1, rows, width)
    hidden_two = hidden_one + gate_one * t_back.astype(jnp.float32)
    cross_in = mover.tick(packed(hidden_two.astype(jnp.bfloat16)))
    mover.finish(c_task)
    c_low, c_high = c_task.state
    w_cquery, w_ckey = columns(c_low, 0, width), columns(c_low, width, width)
    w_cvalue, w_cproj = columns(c_high, 0, width), columns(c_high, width, width)
    text_packed = packed(text)
    c_query_rows = split_heads((packed_product(cross_in, w_cquery) + vec_float[6]).astype(jnp.bfloat16), heads)
    c_key = split_heads(packed_product(text_packed, w_ckey).astype(jnp.bfloat16), heads)
    c_value = split_heads((packed_product(text_packed, w_cvalue) + vec_float[7]).astype(jnp.bfloat16), heads)
    c_query_rows, c_key, c_value = mover.tick((c_query_rows, c_key, c_value))
    c_mixed, c_total = attend_forward(c_query_rows, c_key, c_value, text_mask, CROSS)
    c_flat = mover.tick(packed(merge_heads(c_mixed)))
    hidden_three = hidden_two + (packed_product(c_flat, w_cproj) + vec_float[8])
    normed_two = packed(modulate(hidden_three, mod_table[:, 3], mod_table[:, 4]).astype(jnp.bfloat16))
    normed_two = mover.tick(normed_two)
    mover.finish(i_task)
    inner_act = jnp.concatenate([packed_product(normed_two, part) for part in i_task.state], axis=-1)
    inner_act = inner_act + vec_float[16:].reshape(-1)
    gelu_out = mover.tick(jax.nn.gelu(inner_act, approximate=True).astype(jnp.bfloat16))
    mover.drain()
    w_out = o_task.state
    mlp_branch = product(gelu_out, w_out) + vec_float[9]
    hidden_four = hidden_three + gate_two * mlp_branch

    def pair(arr):
        flat = arr.reshape(-1, arr.shape[-1])
        return jnp.concatenate([flat, swap(flat, "k")], axis=0)

    def pair_packed(arr):
        flat = arr.reshape(-1, arr.shape[-1])
        other = swap(flat, "k")
        half = flat.shape[1] // 2
        return jnp.concatenate([flat, jnp.concatenate([other[:, half:], other[:, :half]], axis=1)], axis=0)

    def choose(low, high):
        return jnp.where(k == 0, low, high)

    def sums_of(left, right):
        return lax.dot_general(left, right, (((0,), (0,)), ((), ())), preferred_element_type=jnp.float32).astype(
            jnp.bfloat16
        )

    grad_mlp = (out_rows * gate_two).astype(jnp.bfloat16)
    grad_gate_two = jnp.sum(out_rows * mlp_branch, axis=1)
    pair_mlp = pair(grad_mlp)
    sum_out = sums_of(pair(gelu_out), choose(pair_mlp[:, :640], pair_mlp[:, 512:]))
    bias_out = column_sum(grad_mlp)
    grad_gelu, sum_out = lax.optimization_barrier((product_back(grad_mlp, w_out), sum_out))
    own_out = mover.add(scatter_out_steps(at), sum_out)
    gelu_pull = jax.vjp(partial(jax.nn.gelu, approximate=True), inner_act)[1]
    grad_inner = mover.tick(gelu_pull(grad_gelu)[0].astype(jnp.bfloat16))
    pair_inner = pair(grad_inner)
    pair_two, inner_half = pair_packed(normed_two), choose(pair_inner[:, :HALF], pair_inner[:, HALF:])
    sum_in = (sums_of(pair_two, inner_half[:, :width]), sums_of(pair_two, inner_half[:, width:]))
    bias_in = column_sum(grad_inner)
    grad_inner, sum_in = mover.tick((grad_inner, sum_in))
    own_in = mover.add(scatter_steps(k), sum_in)
    norm_pull = jax.vjp(modulate, hidden_three, mod_table[:, 3], mod_table[:, 4])[1]
    in_low, in_high = i_task.state
    grad_normed = packed_back(grad_inner[..., :HALF], in_low) + packed_back(grad_inner[..., HALF:], in_high)
    grad_normed = mover.tick(grad_normed)
    grad_three, grad_shift_two, grad_scale_two = norm_pull(unpacked_float(grad_normed))
    grad_three = out_rows + grad_three
    grad_cross = grad_three.astype(jnp.bfloat16)
    bias_cproj = column_sum(grad_cross)
    grad_cmixed = unpacked(packed_back(grad_cross, w_cproj).astype(jnp.bfloat16))
    grad_cmixed = mover.tick(split_heads(grad_cmixed, heads))
    cq_grad, ck_grad, cv_grad = attend_backward(
        c_query_rows, c_key, c_value, text_mask, c_total, grad_cmixed, CROSS
    )
    grad_cquery = merge_heads(cq_grad).astype(jnp.bfloat16)
    grad_key, grad_value = merge_heads(ck_grad).astype(jnp.bfloat16), merge_heads(cv_grad).astype(jnp.bfloat16)
    grad_cquery, grad_key, grad_value = mover.tick((grad_cquery, grad_key, grad_value))
    bias_cquery = column_sum(grad_cquery)
    grad_two = grad_three + unpacked_float(packed_back(grad_cquery, w_cquery))
    bias_cvalue = column_sum(grad_value)
    text_part = unpacked_float(packed_back(grad_key, w_ckey) + packed_back(grad_value, w_cvalue))
    text_two = jnp.concatenate([text_packed[0], text_packed[0]], axis=0)
    sum_kv = sums_of(text_two, choose(pair(grad_key), pair(grad_value)))
    sum_side = sums_of(choose(pair_packed(cross_in), pair_packed(c_flat)), choose(pair(grad_cquery), pair(grad_cross)))
    sum_cross = (choose(sum_side, sum_kv), choose(sum_kv, sum_side))
    grad_temporal = (grad_two * gate_one).astype(jnp.bfloat16).reshape(1, frame_count, patch_count, width)
    grad_temporal, sum_cross = mover.tick((grad_temporal, sum_cross))
    own_cross = mover.add(scatter_steps(k), sum_cross)
    grad_gate_one = jnp.sum(grad_two * t_back.astype(jnp.float32), axis=1)
    grad_places = lax.all_to_all(grad_temporal, "seq", split_axis=2, concat_axis=1, tiled=True)
    bias_tproj = column_sum(grad_places)
    grad_tmixed = unpacked(packed_back(grad_places, t_high).astype(jnp.bfloat16))
    grad_tmixed = mover.tick(split_heads(grad_tmixed, heads))

    def stage_sums(grads, inputs, flat, proj_grad, task):
        query, key, value = mover.tick(tuple(merge_heads(part).astype(jnp.bfloat16) for part in grads))
        pair_in = pair_packed(inputs)
        low = sums_of(pair_in, choose(pair(query), pair(value)))
        high = sums_of(choose(pair_in, pair_packed(flat)), choose(pair(key), pair(proj_grad)))
        query, key, value, low, high = lax.optimization_barrier((query, key, value, low, high))
        owned = mover.add(scatter_steps(k), (low, high))
        mover.tick()
        w_low, w_high = task.state
        back = packed_back(jnp.concatenate([query, key], axis=-1), w_low)
        back = back + packed_back(value, columns(w_high, 0, width))
        return owned, back, column_sum(query), column_sum(value)

    t_grads = attend_backward(*t_parts, None, t_total, grad_tmixed, TEMPORAL)
    own_t, grad_moved, bias_tquery, bias_tvalue = stage_sums(t_grads, moved, t_flat, grad_places, t_task)
    grad_moved = unpacked(grad_moved.astype(jnp.bfloat16))
    grad_moved = mover.tick(grad_moved)
    grad_frames = lax.all_to_all(grad_moved, "seq", split_axis=1, concat_axis=2, tiled=True)
    grad_one = grad_two + grad_frames.astype(jnp.float32).reshape(1, rows, width)
    grad_gate_one = grad_gate_one + jnp.sum(grad_one * s_branch, axis=1)
    grad_spatial = (grad_one * gate_one).astype(jnp.bfloat16).reshape(frame_count, patch_count, width)
    bias_sproj = column_sum(grad_spatial)
    grad_smixed = unpacked(packed_back(grad_spatial, s_high).astype(jnp.bfloat16))
    grad_smixed = mover.tick(split_heads(grad_smixed, heads))
    s_grads = attend_backward(*s_parts, None, s_total, grad_smixed, SPATIAL)
    own_s, grad_normed, bias_squery, bias_svalue = stage_sums(s_grads, frames, s_flat, grad_spatial, s_task)
    grad_normed = mover.tick(grad_normed)
    first_pull = jax.vjp(modulate, hidden, mod_table[:, 0], mod_table[:, 1])[1]
    grad_normed = mover.tick(unpacked_float(grad_normed))
    grad_zero, grad_shift_one, grad_scale_one = first_pull(grad_normed.reshape(1, rows, width))
    grad_input = grad_one + grad_zero
    grad_table = jnp.stack(
        [grad_shift_one, grad_scale_one, grad_gate_one, grad_shift_two, grad_scale_two, grad_gate_two], axis=1
    )[0]
    bias_rows = jnp.stack(
        [
            bias_squery,
            bias_svalue,
            bias_sproj,
            bias_tquery,
            bias_tvalue,
            bias_tproj,
            bias_cquery,
            bias_cvalue,
            bias_cproj,
            bias_out,
        ]
    )
    small = jnp.concatenate([bias_rows, grad_table, bias_in.reshape(4, width)], axis=0)
    small = along_z(sum_over_plane(small)[None])
    vec_grad = lax.dynamic_slice_in_dim(jnp.sum(small, axis=0), shard * ROWS, ROWS, axis=1)
    turned = jnp.stack([lax.dynamic_slice_in_dim(own_embed, (z + 4 - d) % 4, 1, axis=0)[0] for d in range(4)])
    time_grad = lax.dot_general(
        turned.astype(jnp.float32),
        small[:, 10:16].reshape(4, 6 * width),
        (((0,), (0,)), ((), ())),
        precision=HIGHEST,
        preferred_element_type=jnp.float32,
    )
    text_grad = lax.psum_scatter(text_part, "seq", scatter_dimension=2, tiled=True)
    mover.drain()
    grad_s, grad_t, grad_c = own_s.state[None], own_t.state[None], own_cross.state[None]
    return (
        hidden_four.reshape(tokens.shape),
        grad_input.reshape(tokens.shape),
        text_grad,
        time_grad,
        grad_s[..., :3456],
        grad_s[..., 3456:],
        grad_t[..., :3456],
        grad_t[..., 3456:],
        grad_c[..., :1152],
        grad_c[..., 1152:3456],
        grad_c[..., 3456:],
        own_in.state[None],
        own_out.state[None],
        vec_grad[None],
    )


def run_device(sizes, tokens, *rest):
    fits = (sizes["clip"], sizes["seq"]) == (4, 8) and tokens.shape == (1, 2, 256, 1152)
    return (fast_device if fits else per_device)(tokens, *rest)


def solution(mesh):
    placed = (
        P("clip", "seq", None, None),
        P("clip", None, None),
        P(),
        P("clip"),
        P("clip", "seq", None, None),
        P(("clip", "seq"), None),
        P(None, ("clip", "seq"), None),
        P(None, ("clip", "seq"), None),
        P(None, ("clip", "seq"), None),
        P(None, ("clip", "seq"), None),
        P(None, ("clip", "seq"), None),
        P(None, ("clip", "seq"), None),
        P(None, ("clip", "seq"), None),
        P(None, ("clip", "seq"), None),
        P(None, ("clip", "seq"), None),
        P(None, None, ("clip", "seq")),
    )
    return jax.shard_map(
        partial(run_device, dict(mesh.shape)),
        mesh=mesh,
        in_specs=placed,
        out_specs=(
            P("clip", "seq", None, None),
            P("clip", "seq", None, None),
            P("clip", None, "seq"),
            P(("clip", "seq"), None),
            P(None, ("clip", "seq"), None),
            P(None, ("clip", "seq"), None),
            P(None, ("clip", "seq"), None),
            P(None, ("clip", "seq"), None),
            P(None, ("clip", "seq"), None),
            P(None, ("clip", "seq"), None),
            P(None, ("clip", "seq"), None),
            P(None, ("clip", "seq"), None),
            P(None, ("clip", "seq"), None),
            P(None, None, ("clip", "seq")),
        ),
        check_vma=False,
    )
```

```python
from functools import partial
import math

import jax
import jax.numpy as jnp
from jax import lax
from jax.sharding import PartitionSpec as P

HEADS = 16


EPSILON = 1e-06
HIGHEST = lax.Precision.HIGHEST
SPATIAL = ("bqhe", "bkhe", "bhqk")
TEMPORAL = ("cqphe", "ckphe", "cphqk")
CROSS = ("cqhe", "ckhe", "chqk")


def product(left_arr, right_arr):
    return lax.dot_general(
        left_arr,
        right_arr,
        (((left_arr.ndim - 1,), (0,)), ((), ())),
        preferred_element_type=jnp.float32,
    )


def product_back(grad_arr, weight):
    return lax.dot_general(
        grad_arr,
        weight,
        (((grad_arr.ndim - 1,), (1,)), ((), ())),
        preferred_element_type=jnp.float32,
    )


def outer_sum(left_arr, right_arr):
    left_rows = left_arr.reshape(-1, left_arr.shape[-1])
    right_rows = right_arr.reshape(-1, right_arr.shape[-1])
    return lax.dot_general(
        left_rows, right_rows, (((0,), (0,)), ((), ())), preferred_element_type=jnp.float32
    )


def column_sum(grad_arr):
    return jnp.sum(grad_arr.astype(jnp.float32).reshape(-1, grad_arr.shape[-1]), axis=0)


def timestep_embed(step_values, model_width):
    half_width = model_width // 2
    frequency = jnp.exp(-math.log(10000.0) * jnp.arange(half_width, dtype=jnp.float32) / half_width)
    angles = step_values.astype(jnp.float32)[:, None] * frequency[None, :]
    return jnp.concatenate([jnp.cos(angles), jnp.sin(angles)], axis=-1)


def modulate(hidden, shift_row, scale_row):
    centered = hidden - jnp.mean(hidden, axis=-1, keepdims=True)
    normed = centered * lax.rsqrt(jnp.mean(centered * centered, axis=-1, keepdims=True) + EPSILON)
    return normed * (1.0 + scale_row[:, None, :]) + shift_row[:, None, :]


def split_heads(packed_arr, heads):
    return packed_arr.reshape(packed_arr.shape[:-1] + (heads, packed_arr.shape[-1] // heads))


def merge_heads(head_arr):
    return head_arr.reshape(head_arr.shape[:-2] + (head_arr.shape[-2] * head_arr.shape[-1],))


def attend_scores(queries, key_rows, key_mask, forms):
    query_form, key_form, score_form = forms
    scale_factor = queries.shape[-1] ** (-0.5)
    scores = (
        jnp.einsum(
            query_form + "," + key_form + "->" + score_form,
            queries,
            key_rows,
            preferred_element_type=jnp.float32,
        )
        * scale_factor
    )
    if key_mask is not None:
        scores = jnp.where(key_mask, scores, -1000000000.0)
    return scores


def attend_forward(queries, key_rows, values, key_mask, forms):
    query_form, key_form, score_form = forms
    scores = attend_scores(queries, key_rows, key_mask, forms)
    top_score = jnp.max(scores, axis=-1, keepdims=True)
    log_total = top_score + jnp.log(jnp.sum(jnp.exp(scores - top_score), axis=-1, keepdims=True))
    attn_probs = jnp.exp(scores - log_total).astype(jnp.bfloat16)
    mixed_heads = jnp.einsum(
        score_form + "," + key_form + "->" + query_form,
        attn_probs,
        values,
        preferred_element_type=jnp.float32,
    )
    return (mixed_heads.astype(jnp.bfloat16), log_total)


def attend_backward(queries, key_rows, values, key_mask, log_total, grad_mixed, forms):
    query_form, key_form, score_form = forms
    scale_factor = queries.shape[-1] ** (-0.5)
    scores = attend_scores(queries, key_rows, key_mask, forms)
    attn_probs = jnp.exp(scores - log_total)
    grad_probs = jnp.einsum(
        query_form + "," + key_form + "->" + score_form,
        grad_mixed,
        values,
        preferred_element_type=jnp.float32,
    )
    inner_dot = jnp.sum(attn_probs * grad_probs, axis=-1, keepdims=True)
    grad_scores = (attn_probs * (grad_probs - inner_dot)).astype(jnp.bfloat16)
    grad_values = jnp.einsum(
        score_form + "," + query_form + "->" + key_form,
        attn_probs.astype(jnp.bfloat16),
        grad_mixed,
        preferred_element_type=jnp.float32,
    )
    grad_queries = (
        jnp.einsum(
            score_form + "," + key_form + "->" + query_form,
            grad_scores,
            key_rows,
            preferred_element_type=jnp.float32,
        )
        * scale_factor
    )
    grad_keys = (
        jnp.einsum(
            score_form + "," + query_form + "->" + key_form,
            grad_scores,
            queries,
            preferred_element_type=jnp.float32,
        )
        * scale_factor
    )
    return (grad_queries, grad_keys, grad_values)


def project_qkv(inputs, weight, query_bias, value_bias, heads):
    model_width = query_bias.shape[0]
    bias_row = jnp.concatenate([query_bias, jnp.zeros_like(query_bias), value_bias]).astype(
        jnp.float32
    )
    packed = (product(inputs, weight) + bias_row).astype(jnp.bfloat16)
    return (
        split_heads(packed[..., :model_width], heads),
        split_heads(packed[..., model_width : 2 * model_width], heads),
        split_heads(packed[..., 2 * model_width :], heads),
    )


def qkv_backward(grad_parts, inputs, weight):
    model_width = weight.shape[0]
    packed_grad = jnp.concatenate(
        [merge_heads(grad_part) for grad_part in grad_parts], axis=-1
    ).astype(jnp.bfloat16)
    return (
        outer_sum(inputs, packed_grad),
        product_back(packed_grad, weight),
        column_sum(packed_grad[..., :model_width]),
        column_sum(packed_grad[..., 2 * model_width :]),
    )


def layer_forward(hidden, layer_mats, modulation, text, text_mask, heads, frame_count):
    w_sqkv, w_sproj, w_tqkv, w_tproj, w_cquery, w_ckv, w_cproj, w_in, w_out, vec_rows = layer_mats
    clip_count, row_count, model_width = hidden.shape
    patch_count = row_count // frame_count
    vec_float = vec_rows.astype(jnp.float32)
    mod_table = modulation + vec_float[10:16][None]
    gate_one = mod_table[:, None, 2]
    normed = (
        modulate(hidden, mod_table[:, 0], mod_table[:, 1])
        .astype(jnp.bfloat16)
        .reshape(clip_count * frame_count, patch_count, model_width)
    )
    s_query, s_key, s_value = project_qkv(normed, w_sqkv, vec_rows[0], vec_rows[1], heads)
    s_mixed, s_total = attend_forward(s_query, s_key, s_value, None, SPATIAL)
    s_flat = merge_heads(s_mixed)
    s_branch = (product(s_flat, w_sproj) + vec_float[2]).reshape(clip_count, row_count, model_width)
    hidden_one = hidden + gate_one * s_branch
    frames_view = hidden_one.astype(jnp.bfloat16).reshape(
        clip_count, frame_count, patch_count, model_width
    )
    moved = lax.all_to_all(frames_view, "seq", split_axis=2, concat_axis=1, tiled=True)
    t_query, t_key, t_value = project_qkv(moved, w_tqkv, vec_rows[3], vec_rows[4], heads)
    t_mixed, t_total = attend_forward(t_query, t_key, t_value, None, TEMPORAL)
    t_flat = merge_heads(t_mixed)
    t_branch = (product(t_flat, w_tproj) + vec_float[5]).astype(jnp.bfloat16)
    t_back = lax.all_to_all(t_branch, "seq", split_axis=1, concat_axis=2, tiled=True).reshape(
        clip_count, row_count, model_width
    )
    hidden_two = hidden_one + gate_one * t_back.astype(jnp.float32)
    cross_in = hidden_two.astype(jnp.bfloat16)
    c_query = split_heads((product(cross_in, w_cquery) + vec_float[6]).astype(jnp.bfloat16), heads)
    kv_bias = jnp.concatenate([jnp.zeros_like(vec_float[7]), vec_float[7]])
    c_packed = (product(text, w_ckv) + kv_bias).astype(jnp.bfloat16)
    c_key = split_heads(c_packed[..., :model_width], heads)
    c_value = split_heads(c_packed[..., model_width:], heads)
    c_mixed, c_total = attend_forward(c_query, c_key, c_value, text_mask, CROSS)
    c_flat = merge_heads(c_mixed)
    hidden_three = hidden_two + (product(c_flat, w_cproj) + vec_float[8])
    normed_two = modulate(hidden_three, mod_table[:, 3], mod_table[:, 4]).astype(jnp.bfloat16)
    inner_act = product(normed_two, w_in) + vec_float[16:].reshape(-1)
    gelu_out = jax.nn.gelu(inner_act, approximate=True).astype(jnp.bfloat16)
    mlp_branch = product(gelu_out, w_out) + vec_float[9]
    hidden_four = hidden_three + mod_table[:, None, 5] * mlp_branch
    saved = dict(
        mod_table=mod_table,
        hidden=hidden,
        normed=normed,
        s_query=s_query,
        s_key=s_key,
        s_value=s_value,
        s_total=s_total,
        s_flat=s_flat,
        s_branch=s_branch,
        moved=moved,
        t_query=t_query,
        t_key=t_key,
        t_value=t_value,
        t_total=t_total,
        t_flat=t_flat,
        t_back=t_back,
        cross_in=cross_in,
        c_query=c_query,
        c_key=c_key,
        c_value=c_value,
        c_total=c_total,
        c_flat=c_flat,
        hidden_three=hidden_three,
        normed_two=normed_two,
        inner_act=inner_act,
        gelu_out=gelu_out,
        mlp_branch=mlp_branch,
    )
    return (hidden_four, saved)


def layer_backward(grad_hidden, saved, layer_mats, text, text_mask, heads, frame_count):
    w_sqkv, w_sproj, w_tqkv, w_tproj, w_cquery, w_ckv, w_cproj, w_in, w_out, vec_rows = layer_mats
    clip_count, row_count, model_width = grad_hidden.shape
    patch_count = row_count // frame_count
    mod_table = saved["mod_table"]
    gate_one = mod_table[:, None, 2]
    gate_two = mod_table[:, None, 5]
    grad_mlp = (grad_hidden * gate_two).astype(jnp.bfloat16)
    grad_gate_two = jnp.sum(grad_hidden * saved["mlp_branch"], axis=1)
    grad_w_out = outer_sum(saved["gelu_out"], grad_mlp)
    bias_out = column_sum(grad_mlp)
    grad_gelu = product_back(grad_mlp, w_out)
    gelu_pull = jax.vjp(partial(jax.nn.gelu, approximate=True), saved["inner_act"])[1]
    grad_inner = gelu_pull(grad_gelu)[0].astype(jnp.bfloat16)
    grad_w_in = outer_sum(saved["normed_two"], grad_inner)
    bias_in = column_sum(grad_inner)
    grad_normed_two = product_back(grad_inner, w_in)
    norm_pull = jax.vjp(modulate, saved["hidden_three"], mod_table[:, 3], mod_table[:, 4])[1]
    grad_three, grad_shift_two, grad_scale_two = norm_pull(grad_normed_two)
    grad_three = grad_hidden + grad_three
    grad_cross = grad_three.astype(jnp.bfloat16)
    grad_w_cproj = outer_sum(saved["c_flat"], grad_cross)
    bias_cproj = column_sum(grad_cross)
    grad_cmixed = split_heads(product_back(grad_cross, w_cproj).astype(jnp.bfloat16), heads)
    cq_grad, ck_grad, cv_grad = attend_backward(
        saved["c_query"],
        saved["c_key"],
        saved["c_value"],
        text_mask,
        saved["c_total"],
        grad_cmixed,
        CROSS,
    )
    grad_cquery = merge_heads(cq_grad).astype(jnp.bfloat16)
    grad_w_cquery = outer_sum(saved["cross_in"], grad_cquery)
    bias_cquery = column_sum(grad_cquery)
    grad_two = grad_three + product_back(grad_cquery, w_cquery)
    grad_kv = jnp.concatenate([merge_heads(ck_grad), merge_heads(cv_grad)], axis=-1).astype(
        jnp.bfloat16
    )
    grad_w_ckv = outer_sum(text, grad_kv)
    bias_cvalue = column_sum(grad_kv[..., model_width:])
    text_part = product_back(grad_kv, w_ckv)
    grad_gate_one = jnp.sum(grad_two * saved["t_back"].astype(jnp.float32), axis=1)
    grad_temporal = (
        (grad_two * gate_one)
        .astype(jnp.bfloat16)
        .reshape(clip_count, frame_count, patch_count, model_width)
    )
    grad_places = lax.all_to_all(grad_temporal, "seq", split_axis=2, concat_axis=1, tiled=True)
    grad_w_tproj = outer_sum(saved["t_flat"], grad_places)
    bias_tproj = column_sum(grad_places)
    grad_tmixed = split_heads(product_back(grad_places, w_tproj).astype(jnp.bfloat16), heads)
    temporal_grads = attend_backward(
        saved["t_query"],
        saved["t_key"],
        saved["t_value"],
        None,
        saved["t_total"],
        grad_tmixed,
        TEMPORAL,
    )
    grad_w_tqkv, grad_moved, bias_tquery, bias_tvalue = qkv_backward(
        temporal_grads, saved["moved"], w_tqkv
    )
    grad_frames = lax.all_to_all(
        grad_moved.astype(jnp.bfloat16), "seq", split_axis=1, concat_axis=2, tiled=True
    )
    grad_one = grad_two + grad_frames.astype(jnp.float32).reshape(
        clip_count, row_count, model_width
    )
    grad_gate_one = grad_gate_one + jnp.sum(grad_one * saved["s_branch"], axis=1)
    grad_spatial = (
        (grad_one * gate_one)
        .astype(jnp.bfloat16)
        .reshape(clip_count * frame_count, patch_count, model_width)
    )
    grad_w_sproj = outer_sum(saved["s_flat"], grad_spatial)
    bias_sproj = column_sum(grad_spatial)
    grad_smixed = split_heads(product_back(grad_spatial, w_sproj).astype(jnp.bfloat16), heads)
    spatial_grads = attend_backward(
        saved["s_query"],
        saved["s_key"],
        saved["s_value"],
        None,
        saved["s_total"],
        grad_smixed,
        SPATIAL,
    )
    grad_w_sqkv, grad_normed, bias_squery, bias_svalue = qkv_backward(
        spatial_grads, saved["normed"], w_sqkv
    )
    first_pull = jax.vjp(modulate, saved["hidden"], mod_table[:, 0], mod_table[:, 1])[1]
    grad_zero, grad_shift_one, grad_scale_one = first_pull(
        grad_normed.reshape(clip_count, row_count, model_width)
    )
    grad_input = grad_one + grad_zero
    grad_table = jnp.stack(
        [
            grad_shift_one,
            grad_scale_one,
            grad_gate_one,
            grad_shift_two,
            grad_scale_two,
            grad_gate_two,
        ],
        axis=1,
    )
    bias_rows = jnp.stack(
        [
            bias_squery,
            bias_svalue,
            bias_sproj,
            bias_tquery,
            bias_tvalue,
            bias_tproj,
            bias_cquery,
            bias_cvalue,
            bias_cproj,
            bias_out,
        ]
    )
    vec_grad = jnp.concatenate(
        [bias_rows, jnp.sum(grad_table, axis=0), bias_in.reshape(-1, model_width)], axis=0
    )
    layer_grads = (
        grad_w_sqkv,
        grad_w_sproj,
        grad_w_tqkv,
        grad_w_tproj,
        grad_w_cquery,
        grad_w_ckv,
        grad_w_cproj,
        grad_w_in,
        grad_w_out,
        vec_grad,
    )
    return (grad_input, layer_grads, text_part, grad_table)


def per_device(
    tokens,
    text,
    timesteps,
    text_counts,
    out_grad,
    time_weight,
    s_qkv,
    s_proj,
    t_qkv,
    t_proj,
    c_query,
    c_kv,
    c_proj,
    mlp_in,
    mlp_out,
    vectors,
):
    clip_count, frame_count, patch_count, model_width = tokens.shape
    layer_count = s_qkv.shape[0]
    heads = HEADS
    clip_first = lax.axis_index("clip") * clip_count
    my_steps = lax.dynamic_slice_in_dim(timesteps, clip_first, clip_count)
    time_embed = jax.nn.silu(timestep_embed(my_steps, model_width)).astype(jnp.bfloat16)
    time_full = lax.all_gather(time_weight, ("clip", "seq"), axis=0, tiled=True)
    modulation = product(time_embed, time_full).reshape(clip_count, 6, model_width)
    text_mask = (jnp.arange(text.shape[1])[None, :] < text_counts[:, None])[:, None, None, :]
    hidden = tokens.astype(jnp.float32).reshape(clip_count, frame_count * patch_count, model_width)
    layer_mats = None
    layer_idx = 0
    layer_mats = (
        lax.all_gather(s_qkv[layer_idx], ("clip", "seq"), axis=0, tiled=True),
        lax.all_gather(s_proj[layer_idx], ("clip", "seq"), axis=0, tiled=True),
        lax.all_gather(t_qkv[layer_idx], ("clip", "seq"), axis=0, tiled=True),
        lax.all_gather(t_proj[layer_idx], ("clip", "seq"), axis=0, tiled=True),
        lax.all_gather(c_query[layer_idx], ("clip", "seq"), axis=0, tiled=True),
        lax.all_gather(c_kv[layer_idx], ("clip", "seq"), axis=0, tiled=True),
        lax.all_gather(c_proj[layer_idx], ("clip", "seq"), axis=0, tiled=True),
        lax.all_gather(mlp_in[layer_idx], ("clip", "seq"), axis=0, tiled=True),
        lax.all_gather(mlp_out[layer_idx], ("clip", "seq"), axis=0, tiled=True),
        lax.all_gather(vectors[layer_idx], ("clip", "seq"), axis=1, tiled=True),
    )
    hidden, saved = layer_forward(
        hidden, layer_mats, modulation, text, text_mask, heads, frame_count
    )
    saved_list = [saved]
    output = hidden.reshape(tokens.shape)
    grad_hidden = out_grad.astype(jnp.float32).reshape(hidden.shape)
    grad_text = jnp.zeros(text.shape, jnp.float32)
    grad_mod = jnp.zeros(modulation.shape, jnp.float32)
    grad_shards = [None] * layer_count
    for layer_idx in reversed(range(layer_count)):
        back_mats = (
            lax.all_gather(s_qkv[layer_idx], ("clip", "seq"), axis=0, tiled=True),
            lax.all_gather(s_proj[layer_idx], ("clip", "seq"), axis=0, tiled=True),
            lax.all_gather(t_qkv[layer_idx], ("clip", "seq"), axis=0, tiled=True),
            lax.all_gather(t_proj[layer_idx], ("clip", "seq"), axis=0, tiled=True),
            lax.all_gather(c_query[layer_idx], ("clip", "seq"), axis=0, tiled=True),
            lax.all_gather(c_kv[layer_idx], ("clip", "seq"), axis=0, tiled=True),
            lax.all_gather(c_proj[layer_idx], ("clip", "seq"), axis=0, tiled=True),
            lax.all_gather(mlp_in[layer_idx], ("clip", "seq"), axis=0, tiled=True),
            lax.all_gather(mlp_out[layer_idx], ("clip", "seq"), axis=0, tiled=True),
            lax.all_gather(vectors[layer_idx], ("clip", "seq"), axis=1, tiled=True),
        )
        grad_hidden, layer_grads, text_part, table_part = layer_backward(
            grad_hidden, saved_list[layer_idx], back_mats, text, text_mask, heads, frame_count
        )
        grad_text = grad_text + text_part
        grad_mod = grad_mod + table_part
        grad_shards[layer_idx] = (
            lax.psum_scatter(layer_grads[0], ("clip", "seq"), scatter_dimension=0, tiled=True),
            lax.psum_scatter(layer_grads[1], ("clip", "seq"), scatter_dimension=0, tiled=True),
            lax.psum_scatter(layer_grads[2], ("clip", "seq"), scatter_dimension=0, tiled=True),
            lax.psum_scatter(layer_grads[3], ("clip", "seq"), scatter_dimension=0, tiled=True),
            lax.psum_scatter(layer_grads[4], ("clip", "seq"), scatter_dimension=0, tiled=True),
            lax.psum_scatter(layer_grads[5], ("clip", "seq"), scatter_dimension=0, tiled=True),
            lax.psum_scatter(layer_grads[6], ("clip", "seq"), scatter_dimension=0, tiled=True),
            lax.psum_scatter(layer_grads[7], ("clip", "seq"), scatter_dimension=0, tiled=True),
            lax.psum_scatter(layer_grads[8], ("clip", "seq"), scatter_dimension=0, tiled=True),
            lax.psum_scatter(layer_grads[9], ("clip", "seq"), scatter_dimension=1, tiled=True),
        )
    grad_flat = grad_mod.reshape(clip_count, 6 * model_width)
    embed_float = time_embed.astype(jnp.float32)
    time_grad = lax.psum_scatter(
        lax.dot_general(
            embed_float,
            grad_flat,
            (((0,), (0,)), ((), ())),
            precision=HIGHEST,
            preferred_element_type=jnp.float32,
        ),
        ("clip", "seq"),
        scatter_dimension=0,
        tiled=True,
    )
    text_grad = lax.psum_scatter(
        grad_text.astype(jnp.bfloat16), "seq", scatter_dimension=2, tiled=True
    ).astype(jnp.float32)
    stacked = [jnp.stack([grad_shards[0][member]]) for member in range(10)]
    return (
        output,
        grad_hidden.reshape(tokens.shape),
        text_grad,
        time_grad,
        stacked[0],
        stacked[1],
        stacked[2],
        stacked[3],
        stacked[4],
        stacked[5],
        stacked[6],
        stacked[7],
        stacked[8],
        stacked[9],
    )


ROWS = 36
PADDED = 40
HALF = 2304
SWAP = {"x": [(i, i ^ 2) for i in range(8)], "y": [(i, i ^ 4) for i in range(8)], "k": [(i, i ^ 1) for i in range(8)]}


def mesh_coords():
    clip_at = lax.axis_index("clip")
    seq_at = lax.axis_index("seq")
    return clip_at, lax.div(seq_at, 4), lax.rem(lax.div(seq_at, 2), 2), lax.rem(seq_at, 2)


def swap(arr, axis):
    return lax.ppermute(arr, "seq", SWAP[axis])


def turn(arr, d):
    return lax.ppermute(arr, "clip", [(i, (i + d) % 4) for i in range(4)])


class Task:
    def __init__(self, steps, state, held):
        self.held = held
        self.steps, self.state, self.at, self.left, self.tied = steps, state, 0, 0, False

    def done(self):
        return self.at == len(self.steps) and not self.left

    def crosses_plane(self):
        return any(step[0] == "plane" for step in self.steps[self.at :])


class Mover:
    def __init__(self):
        self.tasks = []

    def add(self, steps, state, held=False):
        self.tasks.append(Task(steps, state, held))
        return self.tasks[-1]

    def tick(self, values=()):
        arrived = []
        for task in self.tasks:
            task.left = max(task.left - 1, 0)
            if not task.left and not task.tied and (task.at or task.held):
                arrived.append(task)
        values, states = lax.optimization_barrier((values, [task.state for task in arrived]))
        for task, state in zip(arrived, states):
            task.state, task.tied = state, task.at > 0
        busy, turning, hopping = False, False, False
        for task in self.tasks:
            if task.at < len(task.steps) and not task.left:
                kind, ticks, step = task.steps[task.at]
                if not (kind == "plane" and (busy or hopping) or kind == "z" and (turning or task.held and busy)):
                    task.state = step(task.state)
                    task.at, task.left, task.tied = task.at + 1, ticks, False
            kind = task.steps[task.at - 1][0] if task.left else ""
            turning = turning or kind == "z"
            last = task.held and kind == "plane" and not task.crosses_plane()
            busy = busy or kind == "plane" and not last or task.crosses_plane()
            hopping = hopping or last
        return values

    def finish(self, task):
        while not task.done():
            self.tick()

    def drain(self):
        for task in self.tasks:
            self.finish(task)


def row_place(at):
    z, y, x, k = at
    spots = jnp.arange(32 * PADDED)
    row, back = spots % PADDED, (spots // PADDED) % 4
    step_x, step_y, core = (spots // (4 * PADDED)) % 2, (spots // (8 * PADDED)) % 2, spots // (16 * PADDED)
    owner = ((z + 4 - back) % 4) * 8 + (y ^ step_y) * 4 + (x ^ step_x) * 2 + (k ^ core)
    source = jnp.where(row < ROWS, owner * ROWS + row, -1)
    return (jnp.arange(32 * ROWS)[:, None] == source[None, :]).astype(jnp.bfloat16)


def along_z(own):
    return jnp.concatenate([own] + [turn(own, d) for d in (1, 2, 3)], axis=0)


def gather_steps():
    def start(own):
        parts = [own] + [turn(own, d) for d in (1, 2, 3)]
        return tuple(
            jnp.concatenate([part[..., i : i + HALF] for part in parts], axis=0) for i in (0, HALF)
        )

    def first(state):
        low, high = state
        return jnp.concatenate([low, swap(low, "x")], axis=0), high, swap(high, "y")

    def second(state):
        low, high, beside = state
        across = swap(jnp.concatenate([high, beside], axis=0), "x")
        return (
            jnp.concatenate([low, swap(low, "y")], axis=0),
            jnp.concatenate([high, across[:4], beside, across[4:]], axis=0),
        )

    def third(state):
        low, high = (part.reshape(16 * PADDED, HALF) for part in state)
        return (low, swap(low, "k")), (high, swap(high, "k"))

    return [("z", 1, start), ("plane", 1, first), ("plane", 2, second), ("core", 1, third)]


def gather_out_steps(at):
    z, y, x, k = at

    def both(arr, axis, bit, dim):
        other = swap(arr, axis)
        return jnp.concatenate([jnp.where(bit == 0, arr, other), jnp.where(bit == 0, other, arr)], axis=dim)

    def start(own):
        block = along_z(own[None])
        return jnp.concatenate(
            [lax.dynamic_index_in_dim(block, (z + 4 - i) % 4, 0) for i in range(4)], axis=0
        ).reshape(4, 1, 1, 1, 144, 1152)

    def first(block):
        return both(block[..., :72, :], "x", x, 2), both(block[..., 72:, :], "y", y, 1)

    def second(state):
        return both(state[0], "y", y, 1), both(state[1], "x", x, 2)

    def third(state):
        low, high = (both(part, "k", k, 3) for part in state)
        return jnp.concatenate([low, high], axis=4).reshape(32 * 144, 1152)

    return [("z", 1, start), ("plane", 1, first), ("plane", 2, second), ("core", 1, third)]


def to_owner(kept, sent, k):
    other = swap(sent, "k")
    return jnp.where(k == 0, kept, other), jnp.where(k == 0, other, kept)


def scatter_steps(k):
    def first(state):
        low, high = (part.reshape(2, 2, 2, 4, PADDED, HALF // 2) for part in state)
        return low[:, 0] + swap(low[:, 1], "y"), high[:, :, 0] + swap(high[:, :, 1], "x")

    def second(state):
        low, high = state
        return jnp.concatenate(
            [low[:, 0] + swap(low[:, 1], "x"), high[:, 0] + swap(high[:, 1], "y")], axis=-1
        )

    def third(block):
        kept = block[:, 0].astype(jnp.float32)
        for d in (1, 2, 3):
            kept = kept + turn(block[:, d], 4 - d).astype(jnp.float32)
        return kept

    def fourth(kept):
        return jnp.concatenate(to_owner(kept[0], kept[1], k), axis=1)[:ROWS]

    return [("plane", 1, first), ("plane", 1, second), ("z", 2, third), ("core", 1, fourth)]


def scatter_out_steps(at):
    z, y, x, k = at

    def halve(arr, axis, name, bit):
        sent = lax.dynamic_index_in_dim(arr, 1 - bit, axis, keepdims=False)
        return lax.dynamic_index_in_dim(arr, bit, axis, keepdims=False) + swap(sent, name)

    def first(total):
        block = total.reshape(4, 2, 2, 2, 144, 640)
        return halve(block[..., :384], 1, "y", y), halve(block[..., 384:], 2, "x", x)

    def second(state):
        return jnp.concatenate([halve(state[0], 1, "x", x), halve(state[1], 1, "y", y)], axis=-1)

    def third(block):
        kept = lax.dynamic_index_in_dim(block, z, 0, keepdims=False).astype(jnp.float32)
        for d in (1, 2, 3):
            sent = lax.dynamic_index_in_dim(block, (z + d) % 4, 0, keepdims=False)
            kept = kept + turn(sent, d).astype(jnp.float32)
        return kept

    def fourth(kept):
        mine = lax.dynamic_index_in_dim(kept, k, 0, keepdims=False)
        low, high = to_owner(mine, lax.dynamic_index_in_dim(kept, 1 - k, 0, keepdims=False), k)
        return jnp.concatenate([low, high[:, 128:]], axis=1)

    return [("plane", 1, first), ("plane", 1, second), ("z", 2, third), ("core", 1, fourth)]


def sum_over_plane(arr):
    for axis in ("k", "x", "y"):
        arr = arr + swap(arr, axis)
    return arr


def packed_product(packed, weight):
    half = packed.shape[-1] // 2
    return product(packed[..., :half], weight[0]) + product(packed[..., half:], weight[1])


def packed_back(grad_arr, weight):
    return jnp.concatenate([product_back(grad_arr, part) for part in weight], axis=-1)


def columns(weight, first, count):
    return tuple(part[:, first : first + count] for part in weight)


def fast_device(
    tokens,
    text,
    timesteps,
    text_counts,
    out_grad,
    time_weight,
    s_qkv,
    s_proj,
    t_qkv,
    t_proj,
    c_query,
    c_kv,
    c_proj,
    mlp_in,
    mlp_out,
    vectors,
):
    heads = HEADS
    _, frame_count, patch_count, width = tokens.shape
    rows = frame_count * patch_count
    at = mesh_coords()
    z, y, x, k = at
    shard = z * 8 + lax.axis_index("seq")
    place = row_place(at)

    def packed(arr):
        return product(arr, place).astype(jnp.bfloat16)

    def unpacked(arr):
        return lax.dot_general(
            arr,
            place,
            (((arr.ndim - 1,), (1,)), ((), ())),
            preferred_element_type=jnp.float32,
        ).astype(jnp.bfloat16)

    def unpacked_float(arr):
        return lax.dot_general(
            arr,
            place.astype(jnp.float32),
            (((arr.ndim - 1,), (1,)), ((), ())),
            precision=lax.Precision.HIGH,
            preferred_element_type=jnp.float32,
        )

    def shard_of(*weights):
        return jnp.pad(jnp.concatenate([w[0] for w in weights], axis=1), ((0, PADDED - ROWS), (0, 0)))[None]

    mover = Mover()
    s_task = mover.add(gather_steps(), shard_of(s_qkv, s_proj), held=True)
    t_task = mover.add(gather_steps(), shard_of(t_qkv, t_proj), held=True)
    c_task = mover.add(gather_steps(), shard_of(c_query, c_kv, c_proj), held=True)
    i_task = mover.add(gather_steps(), shard_of(mlp_in), held=True)
    o_task = mover.add(gather_out_steps(at), mlp_out[0], held=True)

    embed = jax.nn.silu(timestep_embed(timesteps, width)).astype(jnp.bfloat16)
    own_embed = lax.dynamic_slice_in_dim(embed, shard * ROWS, ROWS, axis=1)
    mod_part = product(own_embed, time_weight)
    own_vec = jnp.pad(vectors[0].astype(jnp.float32), ((0, 0), (0, width - ROWS)))
    own_vec = jnp.roll(own_vec, shard * ROWS, axis=1)
    own_vec = own_vec.reshape(20, width)
    mod_part = mod_part.reshape(4, 6, width)

    def small_part(d):
        return jnp.concatenate([lax.dynamic_index_in_dim(mod_part, (z + d) % 4, 0, keepdims=False), own_vec])

    spread = small_part(0)
    for d in (1, 2, 3):
        spread = spread + turn(small_part(d), d)
    mover.tick()
    for axis in ("k", "x", "y"):
        spread = mover.tick(spread + swap(spread, axis))
    modulation, vec_float = spread[None, :6], spread[6:]
    hidden = tokens.astype(jnp.float32).reshape(1, rows, width)
    out_rows = out_grad.astype(jnp.float32).reshape(1, rows, width)
    text_mask = (jnp.arange(text.shape[1])[None, :] < text_counts[:, None])[:, None, None, :]

    def split_qkv(inputs_packed, task, query_bias, value_bias):
        low, high = task.state
        first = packed_product(inputs_packed, low)
        value = packed_product(inputs_packed, columns(high, 0, width)) + value_bias
        parts = (first[..., :width] + query_bias, first[..., width:], value)
        return tuple(split_heads(part.astype(jnp.bfloat16), heads) for part in parts)

    mod_table = modulation + vec_float[10:16][None]
    gate_one, gate_two = mod_table[:, None, 2], mod_table[:, None, 5]
    mover.finish(s_task)
    normed = modulate(hidden, mod_table[:, 0], mod_table[:, 1]).astype(jnp.bfloat16)
    frames = packed(normed.reshape(frame_count, patch_count, width))
    frames = mover.tick(frames)
    s_parts = mover.tick(split_qkv(frames, s_task, vec_float[0], vec_float[1]))
    s_mixed, s_total = attend_forward(*s_parts, None, SPATIAL)
    s_flat = mover.tick(packed(merge_heads(s_mixed)))
    s_high = columns(s_task.state[1], width, width)
    s_branch = (packed_product(s_flat, s_high) + vec_float[2]).reshape(1, rows, width)
    hidden_one = hidden + gate_one * s_branch
    moved = lax.all_to_all(
        hidden_one.astype(jnp.bfloat16).reshape(1, frame_count, patch_count, width),
        "seq",
        split_axis=2,
        concat_axis=1,
        tiled=True,
    )
    moved = mover.tick(packed(moved))
    mover.finish(t_task)
    t_parts = mover.tick(split_qkv(moved, t_task, vec_float[3], vec_float[4]))
    t_mixed, t_total = attend_forward(*t_parts, None, TEMPORAL)
    t_flat = mover.tick(packed(merge_heads(t_mixed)))
    t_high = columns(t_task.state[1], width, width)
    t_branch = (packed_product(t_flat, t_high) + vec_float[5]).astype(jnp.bfloat16)
    t_back = lax.all_to_all(t_branch, "seq", split_axis=1, concat_axis=2, tiled=True).reshape(1, rows, width)
    hidden_two = hidden_one + gate_one * t_back.astype(jnp.float32)
    cross_in = mover.tick(packed(hidden_two.astype(jnp.bfloat16)))
    mover.finish(c_task)
    c_low, c_high = c_task.state
    w_cquery, w_ckey = columns(c_low, 0, width), columns(c_low, width, width)
    w_cvalue, w_cproj = columns(c_high, 0, width), columns(c_high, width, width)
    text_packed = packed(text)
    c_query_rows = split_heads((packed_product(cross_in, w_cquery) + vec_float[6]).astype(jnp.bfloat16), heads)
    c_key = split_heads(packed_product(text_packed, w_ckey).astype(jnp.bfloat16), heads)
    c_value = split_heads((packed_product(text_packed, w_cvalue) + vec_float[7]).astype(jnp.bfloat16), heads)
    c_query_rows, c_key, c_value = mover.tick((c_query_rows, c_key, c_value))
    c_mixed, c_total = attend_forward(c_query_rows, c_key, c_value, text_mask, CROSS)
    c_flat = mover.tick(packed(merge_heads(c_mixed)))
    hidden_three = hidden_two + (packed_product(c_flat, w_cproj) + vec_float[8])
    normed_two = packed(modulate(hidden_three, mod_table[:, 3], mod_table[:, 4]).astype(jnp.bfloat16))
    normed_two = mover.tick(normed_two)
    mover.finish(i_task)
    inner_act = jnp.concatenate([packed_product(normed_two, part) for part in i_task.state], axis=-1)
    inner_act = inner_act + vec_float[16:].reshape(-1)
    gelu_out = mover.tick(jax.nn.gelu(inner_act, approximate=True).astype(jnp.bfloat16))
    mover.drain()
    w_out = o_task.state
    mlp_branch = product(gelu_out, w_out) + vec_float[9]
    hidden_four = hidden_three + gate_two * mlp_branch

    def pair(arr):
        flat = arr.reshape(-1, arr.shape[-1])
        return jnp.concatenate([flat, swap(flat, "k")], axis=0)

    def pair_packed(arr):
        flat = arr.reshape(-1, arr.shape[-1])
        other = swap(flat, "k")
        half = flat.shape[1] // 2
        return jnp.concatenate([flat, jnp.concatenate([other[:, half:], other[:, :half]], axis=1)], axis=0)

    def choose(low, high):
        return jnp.where(k == 0, low, high)

    def sums_of(left, right):
        return lax.dot_general(left, right, (((0,), (0,)), ((), ())), preferred_element_type=jnp.float32).astype(
            jnp.bfloat16
        )

    grad_mlp = (out_rows * gate_two).astype(jnp.bfloat16)
    grad_gate_two = jnp.sum(out_rows * mlp_branch, axis=1)
    pair_mlp = pair(grad_mlp)
    sum_out = sums_of(pair(gelu_out), choose(pair_mlp[:, :640], pair_mlp[:, 512:]))
    bias_out = column_sum(grad_mlp)
    grad_gelu, sum_out = lax.optimization_barrier((product_back(grad_mlp, w_out), sum_out))
    own_out = mover.add(scatter_out_steps(at), sum_out)
    gelu_pull = jax.vjp(partial(jax.nn.gelu, approximate=True), inner_act)[1]
    grad_inner = mover.tick(gelu_pull(grad_gelu)[0].astype(jnp.bfloat16))
    pair_inner = pair(grad_inner)
    pair_two, inner_half = pair_packed(normed_two), choose(pair_inner[:, :HALF], pair_inner[:, HALF:])
    sum_in = (sums_of(pair_two, inner_half[:, :width]), sums_of(pair_two, inner_half[:, width:]))
    bias_in = column_sum(grad_inner)
    norm_pull = jax.vjp(modulate, hidden_three, mod_table[:, 3], mod_table[:, 4])[1]
    in_low, in_high = i_task.state
    grad_normed = packed_back(grad_inner[..., :HALF], in_low) + packed_back(grad_inner[..., HALF:], in_high)
    grad_normed, sum_in = lax.optimization_barrier((grad_normed, sum_in))
    own_in = mover.add(scatter_steps(k), sum_in)
    grad_normed = mover.tick(grad_normed)
    grad_three, grad_shift_two, grad_scale_two = norm_pull(unpacked_float(grad_normed))
    grad_three = out_rows + grad_three
    grad_cross = grad_three.astype(jnp.bfloat16)
    bias_cproj = column_sum(grad_cross)
    grad_cmixed = unpacked(packed_back(grad_cross, w_cproj).astype(jnp.bfloat16))
    grad_cmixed = mover.tick(split_heads(grad_cmixed, heads))
    cq_grad, ck_grad, cv_grad = attend_backward(
        c_query_rows, c_key, c_value, text_mask, c_total, grad_cmixed, CROSS
    )
    grad_cquery = merge_heads(cq_grad).astype(jnp.bfloat16)
    grad_key, grad_value = merge_heads(ck_grad).astype(jnp.bfloat16), merge_heads(cv_grad).astype(jnp.bfloat16)
    grad_cquery, grad_key, grad_value = mover.tick((grad_cquery, grad_key, grad_value))
    bias_cquery = column_sum(grad_cquery)
    grad_two = grad_three + unpacked_float(packed_back(grad_cquery, w_cquery))
    bias_cvalue = column_sum(grad_value)
    text_part = unpacked_float(packed_back(grad_key, w_ckey) + packed_back(grad_value, w_cvalue))
    text_two = jnp.concatenate([text_packed[0], text_packed[0]], axis=0)
    sum_kv = sums_of(text_two, choose(pair(grad_key), pair(grad_value)))
    sum_side = sums_of(choose(pair_packed(cross_in), pair_packed(c_flat)), choose(pair(grad_cquery), pair(grad_cross)))
    sum_cross = (choose(sum_side, sum_kv), choose(sum_kv, sum_side))
    grad_temporal = (grad_two * gate_one).astype(jnp.bfloat16).reshape(1, frame_count, patch_count, width)
    grad_temporal, sum_cross = mover.tick((grad_temporal, sum_cross))
    own_cross = mover.add(scatter_steps(k), sum_cross)
    grad_gate_one = jnp.sum(grad_two * t_back.astype(jnp.float32), axis=1)
    grad_places = lax.all_to_all(grad_temporal, "seq", split_axis=2, concat_axis=1, tiled=True)
    bias_tproj = column_sum(grad_places)
    grad_tmixed = unpacked(packed_back(grad_places, t_high).astype(jnp.bfloat16))
    grad_tmixed = mover.tick(split_heads(grad_tmixed, heads))

    def stage_sums(grads, inputs, flat, proj_grad, task):
        query, key, value = mover.tick(tuple(merge_heads(part).astype(jnp.bfloat16) for part in grads))
        pair_in = pair_packed(inputs)
        low = sums_of(pair_in, choose(pair(query), pair(value)))
        high = sums_of(choose(pair_in, pair_packed(flat)), choose(pair(key), pair(proj_grad)))
        w_low, w_high = task.state
        if task is s_task:
            query, key, value, low, high = lax.optimization_barrier((query, key, value, low, high))
            owned = mover.add(scatter_steps(k), (low, high))
            mover.tick()
        back = packed_back(jnp.concatenate([query, key], axis=-1), w_low)
        back = back + packed_back(value, columns(w_high, 0, width))
        if task is t_task:
            back, low, high = lax.optimization_barrier((back, low, high))
            owned = mover.add(scatter_steps(k), (low, high))
        return owned, back, column_sum(query), column_sum(value)

    t_grads = attend_backward(*t_parts, None, t_total, grad_tmixed, TEMPORAL)
    own_t, grad_moved, bias_tquery, bias_tvalue = stage_sums(t_grads, moved, t_flat, grad_places, t_task)
    grad_moved = unpacked(grad_moved.astype(jnp.bfloat16))
    grad_moved = mover.tick(grad_moved)
    grad_frames = lax.all_to_all(grad_moved, "seq", split_axis=1, concat_axis=2, tiled=True)
    grad_one = grad_two + grad_frames.astype(jnp.float32).reshape(1, rows, width)
    grad_gate_one = grad_gate_one + jnp.sum(grad_one * s_branch, axis=1)
    grad_spatial = (grad_one * gate_one).astype(jnp.bfloat16).reshape(frame_count, patch_count, width)
    bias_sproj = column_sum(grad_spatial)
    grad_smixed = unpacked(packed_back(grad_spatial, s_high).astype(jnp.bfloat16))
    grad_smixed = mover.tick(split_heads(grad_smixed, heads))
    s_grads = attend_backward(*s_parts, None, s_total, grad_smixed, SPATIAL)
    own_s, grad_normed, bias_squery, bias_svalue = stage_sums(s_grads, frames, s_flat, grad_spatial, s_task)
    grad_normed = mover.tick(grad_normed)
    first_pull = jax.vjp(modulate, hidden, mod_table[:, 0], mod_table[:, 1])[1]
    grad_normed = mover.tick(unpacked_float(grad_normed))
    grad_zero, grad_shift_one, grad_scale_one = first_pull(grad_normed.reshape(1, rows, width))
    grad_input = grad_one + grad_zero
    grad_table = jnp.stack(
        [grad_shift_one, grad_scale_one, grad_gate_one, grad_shift_two, grad_scale_two, grad_gate_two], axis=1
    )[0]
    bias_rows = jnp.stack(
        [
            bias_squery,
            bias_svalue,
            bias_sproj,
            bias_tquery,
            bias_tvalue,
            bias_tproj,
            bias_cquery,
            bias_cvalue,
            bias_cproj,
            bias_out,
        ]
    )
    small = jnp.concatenate([bias_rows, grad_table, bias_in.reshape(4, width)], axis=0)
    small = along_z(sum_over_plane(small)[None])
    vec_grad = lax.dynamic_slice_in_dim(jnp.sum(small, axis=0), shard * ROWS, ROWS, axis=1)
    turned = jnp.stack([lax.dynamic_slice_in_dim(own_embed, (z + 4 - d) % 4, 1, axis=0)[0] for d in range(4)])
    time_grad = lax.dot_general(
        turned.astype(jnp.float32),
        small[:, 10:16].reshape(4, 6 * width),
        (((0,), (0,)), ((), ())),
        precision=HIGHEST,
        preferred_element_type=jnp.float32,
    )
    text_grad = lax.psum_scatter(text_part, "seq", scatter_dimension=2, tiled=True)
    mover.drain()
    grad_s, grad_t, grad_c = own_s.state[None], own_t.state[None], own_cross.state[None]
    return (
        hidden_four.reshape(tokens.shape),
        grad_input.reshape(tokens.shape),
        text_grad,
        time_grad,
        grad_s[..., :3456],
        grad_s[..., 3456:],
        grad_t[..., :3456],
        grad_t[..., 3456:],
        grad_c[..., :1152],
        grad_c[..., 1152:3456],
        grad_c[..., 3456:],
        own_in.state[None],
        own_out.state[None],
        vec_grad[None],
    )


def run_device(sizes, tokens, *rest):
    fits = (sizes["clip"], sizes["seq"]) == (4, 8) and tokens.shape == (1, 2, 256, 1152)
    return (fast_device if fits else per_device)(tokens, *rest)


def solution(mesh):
    placed = (
        P("clip", "seq", None, None),
        P("clip", None, None),
        P(),
        P("clip"),
        P("clip", "seq", None, None),
        P(("clip", "seq"), None),
        P(None, ("clip", "seq"), None),
        P(None, ("clip", "seq"), None),
        P(None, ("clip", "seq"), None),
        P(None, ("clip", "seq"), None),
        P(None, ("clip", "seq"), None),
        P(None, ("clip", "seq"), None),
        P(None, ("clip", "seq"), None),
        P(None, ("clip", "seq"), None),
        P(None, ("clip", "seq"), None),
        P(None, None, ("clip", "seq")),
    )
    return jax.shard_map(
        partial(run_device, dict(mesh.shape)),
        mesh=mesh,
        in_specs=placed,
        out_specs=(
            P("clip", "seq", None, None),
            P("clip", "seq", None, None),
            P("clip", None, "seq"),
            P(("clip", "seq"), None),
            P(None, ("clip", "seq"), None),
            P(None, ("clip", "seq"), None),
            P(None, ("clip", "seq"), None),
            P(None, ("clip", "seq"), None),
            P(None, ("clip", "seq"), None),
            P(None, ("clip", "seq"), None),
            P(None, ("clip", "seq"), None),
            P(None, ("clip", "seq"), None),
            P(None, ("clip", "seq"), None),
            P(None, None, ("clip", "seq")),
        ),
        check_vma=False,
    )
```

```python
from functools import partial
import math

import jax
import jax.numpy as jnp
from jax import lax
from jax.sharding import PartitionSpec as P

HEADS = 16


EPSILON = 1e-06
HIGHEST = lax.Precision.HIGHEST
SPATIAL = ("bqhe", "bkhe", "bhqk")
TEMPORAL = ("cqphe", "ckphe", "cphqk")
CROSS = ("cqhe", "ckhe", "chqk")


def product(left_arr, right_arr):
    return lax.dot_general(
        left_arr,
        right_arr,
        (((left_arr.ndim - 1,), (0,)), ((), ())),
        preferred_element_type=jnp.float32,
    )


def product_back(grad_arr, weight):
    return lax.dot_general(
        grad_arr,
        weight,
        (((grad_arr.ndim - 1,), (1,)), ((), ())),
        preferred_element_type=jnp.float32,
    )


def outer_sum(left_arr, right_arr):
    left_rows = left_arr.reshape(-1, left_arr.shape[-1])
    right_rows = right_arr.reshape(-1, right_arr.shape[-1])
    return lax.dot_general(
        left_rows, right_rows, (((0,), (0,)), ((), ())), preferred_element_type=jnp.float32
    )


def column_sum(grad_arr):
    return jnp.sum(grad_arr.astype(jnp.float32).reshape(-1, grad_arr.shape[-1]), axis=0)


def timestep_embed(step_values, model_width):
    half_width = model_width // 2
    frequency = jnp.exp(-math.log(10000.0) * jnp.arange(half_width, dtype=jnp.float32) / half_width)
    angles = step_values.astype(jnp.float32)[:, None] * frequency[None, :]
    return jnp.concatenate([jnp.cos(angles), jnp.sin(angles)], axis=-1)


def modulate(hidden, shift_row, scale_row):
    centered = hidden - jnp.mean(hidden, axis=-1, keepdims=True)
    normed = centered * lax.rsqrt(jnp.mean(centered * centered, axis=-1, keepdims=True) + EPSILON)
    return normed * (1.0 + scale_row[:, None, :]) + shift_row[:, None, :]


def split_heads(packed_arr, heads):
    return packed_arr.reshape(packed_arr.shape[:-1] + (heads, packed_arr.shape[-1] // heads))


def merge_heads(head_arr):
    return head_arr.reshape(head_arr.shape[:-2] + (head_arr.shape[-2] * head_arr.shape[-1],))


def attend_scores(queries, key_rows, key_mask, forms):
    query_form, key_form, score_form = forms
    scale_factor = queries.shape[-1] ** (-0.5)
    scores = (
        jnp.einsum(
            query_form + "," + key_form + "->" + score_form,
            queries,
            key_rows,
            preferred_element_type=jnp.float32,
        )
        * scale_factor
    )
    if key_mask is not None:
        scores = jnp.where(key_mask, scores, -1000000000.0)
    return scores


def attend_forward(queries, key_rows, values, key_mask, forms):
    query_form, key_form, score_form = forms
    scores = attend_scores(queries, key_rows, key_mask, forms)
    top_score = jnp.max(scores, axis=-1, keepdims=True)
    log_total = top_score + jnp.log(jnp.sum(jnp.exp(scores - top_score), axis=-1, keepdims=True))
    attn_probs = jnp.exp(scores - log_total).astype(jnp.bfloat16)
    mixed_heads = jnp.einsum(
        score_form + "," + key_form + "->" + query_form,
        attn_probs,
        values,
        preferred_element_type=jnp.float32,
    )
    return (mixed_heads.astype(jnp.bfloat16), log_total)


def attend_backward(queries, key_rows, values, key_mask, log_total, grad_mixed, forms):
    query_form, key_form, score_form = forms
    scale_factor = queries.shape[-1] ** (-0.5)
    scores = attend_scores(queries, key_rows, key_mask, forms)
    attn_probs = jnp.exp(scores - log_total)
    grad_probs = jnp.einsum(
        query_form + "," + key_form + "->" + score_form,
        grad_mixed,
        values,
        preferred_element_type=jnp.float32,
    )
    inner_dot = jnp.sum(attn_probs * grad_probs, axis=-1, keepdims=True)
    grad_scores = (attn_probs * (grad_probs - inner_dot)).astype(jnp.bfloat16)
    grad_values = jnp.einsum(
        score_form + "," + query_form + "->" + key_form,
        attn_probs.astype(jnp.bfloat16),
        grad_mixed,
        preferred_element_type=jnp.float32,
    )
    grad_queries = (
        jnp.einsum(
            score_form + "," + key_form + "->" + query_form,
            grad_scores,
            key_rows,
            preferred_element_type=jnp.float32,
        )
        * scale_factor
    )
    grad_keys = (
        jnp.einsum(
            score_form + "," + query_form + "->" + key_form,
            grad_scores,
            queries,
            preferred_element_type=jnp.float32,
        )
        * scale_factor
    )
    return (grad_queries, grad_keys, grad_values)


def project_qkv(inputs, weight, query_bias, value_bias, heads):
    model_width = query_bias.shape[0]
    bias_row = jnp.concatenate([query_bias, jnp.zeros_like(query_bias), value_bias]).astype(
        jnp.float32
    )
    packed = (product(inputs, weight) + bias_row).astype(jnp.bfloat16)
    return (
        split_heads(packed[..., :model_width], heads),
        split_heads(packed[..., model_width : 2 * model_width], heads),
        split_heads(packed[..., 2 * model_width :], heads),
    )


def qkv_backward(grad_parts, inputs, weight):
    model_width = weight.shape[0]
    packed_grad = jnp.concatenate(
        [merge_heads(grad_part) for grad_part in grad_parts], axis=-1
    ).astype(jnp.bfloat16)
    return (
        outer_sum(inputs, packed_grad),
        product_back(packed_grad, weight),
        column_sum(packed_grad[..., :model_width]),
        column_sum(packed_grad[..., 2 * model_width :]),
    )


def layer_forward(hidden, layer_mats, modulation, text, text_mask, heads, frame_count):
    w_sqkv, w_sproj, w_tqkv, w_tproj, w_cquery, w_ckv, w_cproj, w_in, w_out, vec_rows = layer_mats
    clip_count, row_count, model_width = hidden.shape
    patch_count = row_count // frame_count
    vec_float = vec_rows.astype(jnp.float32)
    mod_table = modulation + vec_float[10:16][None]
    gate_one = mod_table[:, None, 2]
    normed = (
        modulate(hidden, mod_table[:, 0], mod_table[:, 1])
        .astype(jnp.bfloat16)
        .reshape(clip_count * frame_count, patch_count, model_width)
    )
    s_query, s_key, s_value = project_qkv(normed, w_sqkv, vec_rows[0], vec_rows[1], heads)
    s_mixed, s_total = attend_forward(s_query, s_key, s_value, None, SPATIAL)
    s_flat = merge_heads(s_mixed)
    s_branch = (product(s_flat, w_sproj) + vec_float[2]).reshape(clip_count, row_count, model_width)
    hidden_one = hidden + gate_one * s_branch
    frames_view = hidden_one.astype(jnp.bfloat16).reshape(
        clip_count, frame_count, patch_count, model_width
    )
    moved = lax.all_to_all(frames_view, "seq", split_axis=2, concat_axis=1, tiled=True)
    t_query, t_key, t_value = project_qkv(moved, w_tqkv, vec_rows[3], vec_rows[4], heads)
    t_mixed, t_total = attend_forward(t_query, t_key, t_value, None, TEMPORAL)
    t_flat = merge_heads(t_mixed)
    t_branch = (product(t_flat, w_tproj) + vec_float[5]).astype(jnp.bfloat16)
    t_back = lax.all_to_all(t_branch, "seq", split_axis=1, concat_axis=2, tiled=True).reshape(
        clip_count, row_count, model_width
    )
    hidden_two = hidden_one + gate_one * t_back.astype(jnp.float32)
    cross_in = hidden_two.astype(jnp.bfloat16)
    c_query = split_heads((product(cross_in, w_cquery) + vec_float[6]).astype(jnp.bfloat16), heads)
    kv_bias = jnp.concatenate([jnp.zeros_like(vec_float[7]), vec_float[7]])
    c_packed = (product(text, w_ckv) + kv_bias).astype(jnp.bfloat16)
    c_key = split_heads(c_packed[..., :model_width], heads)
    c_value = split_heads(c_packed[..., model_width:], heads)
    c_mixed, c_total = attend_forward(c_query, c_key, c_value, text_mask, CROSS)
    c_flat = merge_heads(c_mixed)
    hidden_three = hidden_two + (product(c_flat, w_cproj) + vec_float[8])
    normed_two = modulate(hidden_three, mod_table[:, 3], mod_table[:, 4]).astype(jnp.bfloat16)
    inner_act = product(normed_two, w_in) + vec_float[16:].reshape(-1)
    gelu_out = jax.nn.gelu(inner_act, approximate=True).astype(jnp.bfloat16)
    mlp_branch = product(gelu_out, w_out) + vec_float[9]
    hidden_four = hidden_three + mod_table[:, None, 5] * mlp_branch
    saved = dict(
        mod_table=mod_table,
        hidden=hidden,
        normed=normed,
        s_query=s_query,
        s_key=s_key,
        s_value=s_value,
        s_total=s_total,
        s_flat=s_flat,
        s_branch=s_branch,
        moved=moved,
        t_query=t_query,
        t_key=t_key,
        t_value=t_value,
        t_total=t_total,
        t_flat=t_flat,
        t_back=t_back,
        cross_in=cross_in,
        c_query=c_query,
        c_key=c_key,
        c_value=c_value,
        c_total=c_total,
        c_flat=c_flat,
        hidden_three=hidden_three,
        normed_two=normed_two,
        inner_act=inner_act,
        gelu_out=gelu_out,
        mlp_branch=mlp_branch,
    )
    return (hidden_four, saved)


def layer_backward(grad_hidden, saved, layer_mats, text, text_mask, heads, frame_count):
    w_sqkv, w_sproj, w_tqkv, w_tproj, w_cquery, w_ckv, w_cproj, w_in, w_out, vec_rows = layer_mats
    clip_count, row_count, model_width = grad_hidden.shape
    patch_count = row_count // frame_count
    mod_table = saved["mod_table"]
    gate_one = mod_table[:, None, 2]
    gate_two = mod_table[:, None, 5]
    grad_mlp = (grad_hidden * gate_two).astype(jnp.bfloat16)
    grad_gate_two = jnp.sum(grad_hidden * saved["mlp_branch"], axis=1)
    grad_w_out = outer_sum(saved["gelu_out"], grad_mlp)
    bias_out = column_sum(grad_mlp)
    grad_gelu = product_back(grad_mlp, w_out)
    gelu_pull = jax.vjp(partial(jax.nn.gelu, approximate=True), saved["inner_act"])[1]
    grad_inner = gelu_pull(grad_gelu)[0].astype(jnp.bfloat16)
    grad_w_in = outer_sum(saved["normed_two"], grad_inner)
    bias_in = column_sum(grad_inner)
    grad_normed_two = product_back(grad_inner, w_in)
    norm_pull = jax.vjp(modulate, saved["hidden_three"], mod_table[:, 3], mod_table[:, 4])[1]
    grad_three, grad_shift_two, grad_scale_two = norm_pull(grad_normed_two)
    grad_three = grad_hidden + grad_three
    grad_cross = grad_three.astype(jnp.bfloat16)
    grad_w_cproj = outer_sum(saved["c_flat"], grad_cross)
    bias_cproj = column_sum(grad_cross)
    grad_cmixed = split_heads(product_back(grad_cross, w_cproj).astype(jnp.bfloat16), heads)
    cq_grad, ck_grad, cv_grad = attend_backward(
        saved["c_query"],
        saved["c_key"],
        saved["c_value"],
        text_mask,
        saved["c_total"],
        grad_cmixed,
        CROSS,
    )
    grad_cquery = merge_heads(cq_grad).astype(jnp.bfloat16)
    grad_w_cquery = outer_sum(saved["cross_in"], grad_cquery)
    bias_cquery = column_sum(grad_cquery)
    grad_two = grad_three + product_back(grad_cquery, w_cquery)
    grad_kv = jnp.concatenate([merge_heads(ck_grad), merge_heads(cv_grad)], axis=-1).astype(
        jnp.bfloat16
    )
    grad_w_ckv = outer_sum(text, grad_kv)
    bias_cvalue = column_sum(grad_kv[..., model_width:])
    text_part = product_back(grad_kv, w_ckv)
    grad_gate_one = jnp.sum(grad_two * saved["t_back"].astype(jnp.float32), axis=1)
    grad_temporal = (
        (grad_two * gate_one)
        .astype(jnp.bfloat16)
        .reshape(clip_count, frame_count, patch_count, model_width)
    )
    grad_places = lax.all_to_all(grad_temporal, "seq", split_axis=2, concat_axis=1, tiled=True)
    grad_w_tproj = outer_sum(saved["t_flat"], grad_places)
    bias_tproj = column_sum(grad_places)
    grad_tmixed = split_heads(product_back(grad_places, w_tproj).astype(jnp.bfloat16), heads)
    temporal_grads = attend_backward(
        saved["t_query"],
        saved["t_key"],
        saved["t_value"],
        None,
        saved["t_total"],
        grad_tmixed,
        TEMPORAL,
    )
    grad_w_tqkv, grad_moved, bias_tquery, bias_tvalue = qkv_backward(
        temporal_grads, saved["moved"], w_tqkv
    )
    grad_frames = lax.all_to_all(
        grad_moved.astype(jnp.bfloat16), "seq", split_axis=1, concat_axis=2, tiled=True
    )
    grad_one = grad_two + grad_frames.astype(jnp.float32).reshape(
        clip_count, row_count, model_width
    )
    grad_gate_one = grad_gate_one + jnp.sum(grad_one * saved["s_branch"], axis=1)
    grad_spatial = (
        (grad_one * gate_one)
        .astype(jnp.bfloat16)
        .reshape(clip_count * frame_count, patch_count, model_width)
    )
    grad_w_sproj = outer_sum(saved["s_flat"], grad_spatial)
    bias_sproj = column_sum(grad_spatial)
    grad_smixed = split_heads(product_back(grad_spatial, w_sproj).astype(jnp.bfloat16), heads)
    spatial_grads = attend_backward(
        saved["s_query"],
        saved["s_key"],
        saved["s_value"],
        None,
        saved["s_total"],
        grad_smixed,
        SPATIAL,
    )
    grad_w_sqkv, grad_normed, bias_squery, bias_svalue = qkv_backward(
        spatial_grads, saved["normed"], w_sqkv
    )
    first_pull = jax.vjp(modulate, saved["hidden"], mod_table[:, 0], mod_table[:, 1])[1]
    grad_zero, grad_shift_one, grad_scale_one = first_pull(
        grad_normed.reshape(clip_count, row_count, model_width)
    )
    grad_input = grad_one + grad_zero
    grad_table = jnp.stack(
        [
            grad_shift_one,
            grad_scale_one,
            grad_gate_one,
            grad_shift_two,
            grad_scale_two,
            grad_gate_two,
        ],
        axis=1,
    )
    bias_rows = jnp.stack(
        [
            bias_squery,
            bias_svalue,
            bias_sproj,
            bias_tquery,
            bias_tvalue,
            bias_tproj,
            bias_cquery,
            bias_cvalue,
            bias_cproj,
            bias_out,
        ]
    )
    vec_grad = jnp.concatenate(
        [bias_rows, jnp.sum(grad_table, axis=0), bias_in.reshape(-1, model_width)], axis=0
    )
    layer_grads = (
        grad_w_sqkv,
        grad_w_sproj,
        grad_w_tqkv,
        grad_w_tproj,
        grad_w_cquery,
        grad_w_ckv,
        grad_w_cproj,
        grad_w_in,
        grad_w_out,
        vec_grad,
    )
    return (grad_input, layer_grads, text_part, grad_table)


def per_device(
    tokens,
    text,
    timesteps,
    text_counts,
    out_grad,
    time_weight,
    s_qkv,
    s_proj,
    t_qkv,
    t_proj,
    c_query,
    c_kv,
    c_proj,
    mlp_in,
    mlp_out,
    vectors,
):
    clip_count, frame_count, patch_count, model_width = tokens.shape
    layer_count = s_qkv.shape[0]
    heads = HEADS
    clip_first = lax.axis_index("clip") * clip_count
    my_steps = lax.dynamic_slice_in_dim(timesteps, clip_first, clip_count)
    time_embed = jax.nn.silu(timestep_embed(my_steps, model_width)).astype(jnp.bfloat16)
    time_full = lax.all_gather(time_weight, ("clip", "seq"), axis=0, tiled=True)
    modulation = product(time_embed, time_full).reshape(clip_count, 6, model_width)
    text_mask = (jnp.arange(text.shape[1])[None, :] < text_counts[:, None])[:, None, None, :]
    hidden = tokens.astype(jnp.float32).reshape(clip_count, frame_count * patch_count, model_width)
    layer_mats = None
    layer_idx = 0
    layer_mats = (
        lax.all_gather(s_qkv[layer_idx], ("clip", "seq"), axis=0, tiled=True),
        lax.all_gather(s_proj[layer_idx], ("clip", "seq"), axis=0, tiled=True),
        lax.all_gather(t_qkv[layer_idx], ("clip", "seq"), axis=0, tiled=True),
        lax.all_gather(t_proj[layer_idx], ("clip", "seq"), axis=0, tiled=True),
        lax.all_gather(c_query[layer_idx], ("clip", "seq"), axis=0, tiled=True),
        lax.all_gather(c_kv[layer_idx], ("clip", "seq"), axis=0, tiled=True),
        lax.all_gather(c_proj[layer_idx], ("clip", "seq"), axis=0, tiled=True),
        lax.all_gather(mlp_in[layer_idx], ("clip", "seq"), axis=0, tiled=True),
        lax.all_gather(mlp_out[layer_idx], ("clip", "seq"), axis=0, tiled=True),
        lax.all_gather(vectors[layer_idx], ("clip", "seq"), axis=1, tiled=True),
    )
    hidden, saved = layer_forward(
        hidden, layer_mats, modulation, text, text_mask, heads, frame_count
    )
    saved_list = [saved]
    output = hidden.reshape(tokens.shape)
    grad_hidden = out_grad.astype(jnp.float32).reshape(hidden.shape)
    grad_text = jnp.zeros(text.shape, jnp.float32)
    grad_mod = jnp.zeros(modulation.shape, jnp.float32)
    grad_shards = [None] * layer_count
    for layer_idx in reversed(range(layer_count)):
        back_mats = (
            lax.all_gather(s_qkv[layer_idx], ("clip", "seq"), axis=0, tiled=True),
            lax.all_gather(s_proj[layer_idx], ("clip", "seq"), axis=0, tiled=True),
            lax.all_gather(t_qkv[layer_idx], ("clip", "seq"), axis=0, tiled=True),
            lax.all_gather(t_proj[layer_idx], ("clip", "seq"), axis=0, tiled=True),
            lax.all_gather(c_query[layer_idx], ("clip", "seq"), axis=0, tiled=True),
            lax.all_gather(c_kv[layer_idx], ("clip", "seq"), axis=0, tiled=True),
            lax.all_gather(c_proj[layer_idx], ("clip", "seq"), axis=0, tiled=True),
            lax.all_gather(mlp_in[layer_idx], ("clip", "seq"), axis=0, tiled=True),
            lax.all_gather(mlp_out[layer_idx], ("clip", "seq"), axis=0, tiled=True),
            lax.all_gather(vectors[layer_idx], ("clip", "seq"), axis=1, tiled=True),
        )
        grad_hidden, layer_grads, text_part, table_part = layer_backward(
            grad_hidden, saved_list[layer_idx], back_mats, text, text_mask, heads, frame_count
        )
        grad_text = grad_text + text_part
        grad_mod = grad_mod + table_part
        grad_shards[layer_idx] = (
            lax.psum_scatter(layer_grads[0], ("clip", "seq"), scatter_dimension=0, tiled=True),
            lax.psum_scatter(layer_grads[1], ("clip", "seq"), scatter_dimension=0, tiled=True),
            lax.psum_scatter(layer_grads[2], ("clip", "seq"), scatter_dimension=0, tiled=True),
            lax.psum_scatter(layer_grads[3], ("clip", "seq"), scatter_dimension=0, tiled=True),
            lax.psum_scatter(layer_grads[4], ("clip", "seq"), scatter_dimension=0, tiled=True),
            lax.psum_scatter(layer_grads[5], ("clip", "seq"), scatter_dimension=0, tiled=True),
            lax.psum_scatter(layer_grads[6], ("clip", "seq"), scatter_dimension=0, tiled=True),
            lax.psum_scatter(layer_grads[7], ("clip", "seq"), scatter_dimension=0, tiled=True),
            lax.psum_scatter(layer_grads[8], ("clip", "seq"), scatter_dimension=0, tiled=True),
            lax.psum_scatter(layer_grads[9], ("clip", "seq"), scatter_dimension=1, tiled=True),
        )
    grad_flat = grad_mod.reshape(clip_count, 6 * model_width)
    embed_float = time_embed.astype(jnp.float32)
    time_grad = lax.psum_scatter(
        lax.dot_general(
            embed_float,
            grad_flat,
            (((0,), (0,)), ((), ())),
            precision=HIGHEST,
            preferred_element_type=jnp.float32,
        ),
        ("clip", "seq"),
        scatter_dimension=0,
        tiled=True,
    )
    text_grad = lax.psum_scatter(
        grad_text.astype(jnp.bfloat16), "seq", scatter_dimension=2, tiled=True
    ).astype(jnp.float32)
    stacked = [jnp.stack([grad_shards[0][member]]) for member in range(10)]
    return (
        output,
        grad_hidden.reshape(tokens.shape),
        text_grad,
        time_grad,
        stacked[0],
        stacked[1],
        stacked[2],
        stacked[3],
        stacked[4],
        stacked[5],
        stacked[6],
        stacked[7],
        stacked[8],
        stacked[9],
    )


ROWS = 36
PADDED = 40
HALF = 2304
SWAP = {"x": [(i, i ^ 2) for i in range(8)], "y": [(i, i ^ 4) for i in range(8)], "k": [(i, i ^ 1) for i in range(8)]}


def mesh_coords():
    clip_at = lax.axis_index("clip")
    seq_at = lax.axis_index("seq")
    return clip_at, lax.div(seq_at, 4), lax.rem(lax.div(seq_at, 2), 2), lax.rem(seq_at, 2)


def swap(arr, axis):
    return lax.ppermute(arr, "seq", SWAP[axis])


def turn(arr, d):
    return lax.ppermute(arr, "clip", [(i, (i + d) % 4) for i in range(4)])


class Task:
    def __init__(self, steps, state, held):
        self.held = held
        self.steps, self.state, self.at, self.left, self.tied = steps, state, 0, 0, False

    def done(self):
        return self.at == len(self.steps) and not self.left

    def crosses_plane(self):
        return any(step[0] == "plane" for step in self.steps[self.at :])


class Mover:
    def __init__(self):
        self.tasks = []

    def add(self, steps, state, held=False):
        self.tasks.append(Task(steps, state, held))
        return self.tasks[-1]

    def tick(self, values=()):
        arrived = []
        for task in self.tasks:
            task.left = max(task.left - 1, 0)
            if not task.left and not task.tied and (task.at or task.held):
                arrived.append(task)
        values, states = lax.optimization_barrier((values, [task.state for task in arrived]))
        for task, state in zip(arrived, states):
            task.state, task.tied = state, task.at > 0
        busy, turning, hopping = False, False, False
        for task in self.tasks:
            if task.at < len(task.steps) and not task.left:
                kind, ticks, step = task.steps[task.at]
                if not (kind == "plane" and (busy or hopping) or kind == "z" and (turning or task.held and busy)):
                    task.state = step(task.state)
                    task.at, task.left, task.tied = task.at + 1, ticks, False
            kind = task.steps[task.at - 1][0] if task.left else ""
            turning = turning or kind == "z"
            last = task.held and kind == "plane" and not task.crosses_plane()
            busy = busy or kind == "plane" and not last or task.crosses_plane()
            hopping = hopping or last
        return values

    def finish(self, task):
        while not task.done():
            self.tick()

    def drain(self):
        for task in self.tasks:
            self.finish(task)


def row_place(at):
    z, y, x, k = at
    spots = jnp.arange(32 * PADDED)
    row, back = spots % PADDED, (spots // PADDED) % 4
    step_x, step_y, core = (spots // (4 * PADDED)) % 2, (spots // (8 * PADDED)) % 2, spots // (16 * PADDED)
    owner = ((z + 4 - back) % 4) * 8 + (y ^ step_y) * 4 + (x ^ step_x) * 2 + (k ^ core)
    source = jnp.where(row < ROWS, owner * ROWS + row, -1)
    return (jnp.arange(32 * ROWS)[:, None] == source[None, :]).astype(jnp.bfloat16)


def along_z(own):
    return jnp.concatenate([own] + [turn(own, d) for d in (1, 2, 3)], axis=0)


def gather_steps():
    def start(own):
        parts = [own] + [turn(own, d) for d in (1, 2, 3)]
        return tuple(
            jnp.concatenate([part[..., i : i + HALF] for part in parts], axis=0) for i in (0, HALF)
        )

    def first(state):
        low, high = state
        return jnp.concatenate([low, swap(low, "x")], axis=0), high, swap(high, "y")

    def second(state):
        low, high, beside = state
        across = swap(jnp.concatenate([high, beside], axis=0), "x")
        return (
            jnp.concatenate([low, swap(low, "y")], axis=0),
            jnp.concatenate([high, across[:4], beside, across[4:]], axis=0),
        )

    def third(state):
        low, high = (part.reshape(16 * PADDED, HALF) for part in state)
        return (low, swap(low, "k")), (high, swap(high, "k"))

    return [("z", 1, start), ("plane", 1, first), ("plane", 2, second), ("core", 1, third)]


def gather_out_steps(at):
    z, y, x, k = at

    def both(arr, axis, bit, dim):
        other = swap(arr, axis)
        return jnp.concatenate([jnp.where(bit == 0, arr, other), jnp.where(bit == 0, other, arr)], axis=dim)

    def start(own):
        block = along_z(own[None])
        return jnp.concatenate(
            [lax.dynamic_index_in_dim(block, (z + 4 - i) % 4, 0) for i in range(4)], axis=0
        ).reshape(4, 1, 1, 1, 144, 1152)

    def first(block):
        return both(block[..., :72, :], "x", x, 2), both(block[..., 72:, :], "y", y, 1)

    def second(state):
        return both(state[0], "y", y, 1), both(state[1], "x", x, 2)

    def third(state):
        low, high = (both(part, "k", k, 3) for part in state)
        return jnp.concatenate([low, high], axis=4).reshape(32 * 144, 1152)

    return [("z", 1, start), ("plane", 1, first), ("plane", 2, second), ("core", 1, third)]


def to_owner(kept, sent, k):
    other = swap(sent, "k")
    return jnp.where(k == 0, kept, other), jnp.where(k == 0, other, kept)


def scatter_steps(k):
    def first(state):
        low, high = (part.reshape(2, 2, 2, 4, PADDED, HALF // 2) for part in state)
        return low[:, 0] + swap(low[:, 1], "y"), high[:, :, 0] + swap(high[:, :, 1], "x")

    def second(state):
        low, high = state
        return jnp.concatenate(
            [low[:, 0] + swap(low[:, 1], "x"), high[:, 0] + swap(high[:, 1], "y")], axis=-1
        )

    def third(block):
        kept = block[:, 0].astype(jnp.float32)
        for d in (1, 2, 3):
            kept = kept + turn(block[:, d], 4 - d).astype(jnp.float32)
        return kept

    def fourth(kept):
        return jnp.concatenate(to_owner(kept[0], kept[1], k), axis=1)[:ROWS]

    return [("plane", 1, first), ("plane", 1, second), ("z", 2, third), ("core", 1, fourth)]


def scatter_out_steps(at):
    z, y, x, k = at

    def halve(arr, axis, name, bit):
        sent = lax.dynamic_index_in_dim(arr, 1 - bit, axis, keepdims=False)
        return lax.dynamic_index_in_dim(arr, bit, axis, keepdims=False) + swap(sent, name)

    def first(total):
        block = total.reshape(4, 2, 2, 2, 144, 640)
        return halve(block[..., :384], 1, "y", y), halve(block[..., 384:], 2, "x", x)

    def second(state):
        return jnp.concatenate([halve(state[0], 1, "x", x), halve(state[1], 1, "y", y)], axis=-1)

    def third(block):
        kept = lax.dynamic_index_in_dim(block, z, 0, keepdims=False).astype(jnp.float32)
        for d in (1, 2, 3):
            sent = lax.dynamic_index_in_dim(block, (z + d) % 4, 0, keepdims=False)
            kept = kept + turn(sent, d).astype(jnp.float32)
        return kept

    def fourth(kept):
        mine = lax.dynamic_index_in_dim(kept, k, 0, keepdims=False)
        low, high = to_owner(mine, lax.dynamic_index_in_dim(kept, 1 - k, 0, keepdims=False), k)
        return jnp.concatenate([low, high[:, 128:]], axis=1)

    return [("plane", 1, first), ("plane", 1, second), ("z", 2, third), ("core", 1, fourth)]


def sum_over_plane(arr):
    for axis in ("k", "x", "y"):
        arr = arr + swap(arr, axis)
    return arr


def packed_product(packed, weight):
    half = packed.shape[-1] // 2
    return product(packed[..., :half], weight[0]) + product(packed[..., half:], weight[1])


def packed_back(grad_arr, weight):
    return jnp.concatenate([product_back(grad_arr, part) for part in weight], axis=-1)


def columns(weight, first, count):
    return tuple(part[:, first : first + count] for part in weight)


def fast_device(
    tokens,
    text,
    timesteps,
    text_counts,
    out_grad,
    time_weight,
    s_qkv,
    s_proj,
    t_qkv,
    t_proj,
    c_query,
    c_kv,
    c_proj,
    mlp_in,
    mlp_out,
    vectors,
):
    heads = HEADS
    _, frame_count, patch_count, width = tokens.shape
    rows = frame_count * patch_count
    at = mesh_coords()
    z, y, x, k = at
    shard = z * 8 + lax.axis_index("seq")
    place = row_place(at)

    def packed(arr):
        return product(arr, place).astype(jnp.bfloat16)

    def unpacked(arr):
        return lax.dot_general(
            arr,
            place,
            (((arr.ndim - 1,), (1,)), ((), ())),
            preferred_element_type=jnp.float32,
        ).astype(jnp.bfloat16)

    def unpacked_float(arr):
        return lax.dot_general(
            arr,
            place.astype(jnp.float32),
            (((arr.ndim - 1,), (1,)), ((), ())),
            precision=lax.Precision.HIGH,
            preferred_element_type=jnp.float32,
        )

    def shard_of(*weights):
        return jnp.pad(jnp.concatenate([w[0] for w in weights], axis=1), ((0, PADDED - ROWS), (0, 0)))[None]

    mover = Mover()
    s_task = mover.add(gather_steps(), shard_of(s_qkv, s_proj), held=True)
    t_task = mover.add(gather_steps(), shard_of(t_qkv, t_proj), held=True)
    c_task = mover.add(gather_steps(), shard_of(c_query, c_kv, c_proj), held=True)
    i_task = mover.add(gather_steps(), shard_of(mlp_in), held=True)
    o_task = mover.add(gather_out_steps(at), mlp_out[0], held=True)

    embed = jax.nn.silu(timestep_embed(timesteps, width)).astype(jnp.bfloat16)
    own_embed = lax.dynamic_slice_in_dim(embed, shard * ROWS, ROWS, axis=1)
    mod_part = product(own_embed, time_weight)
    own_vec = jnp.pad(vectors[0].astype(jnp.float32), ((0, 0), (0, width - ROWS)))
    own_vec = jnp.roll(own_vec, shard * ROWS, axis=1)
    own_vec = own_vec.reshape(20, width)
    mod_part = mod_part.reshape(4, 6, width)

    def small_part(d):
        return jnp.concatenate([lax.dynamic_index_in_dim(mod_part, (z + d) % 4, 0, keepdims=False), own_vec])

    spread = small_part(0)
    for d in (1, 2, 3):
        spread = spread + turn(small_part(d), d)
    mover.tick()
    for axis in ("k", "x", "y"):
        spread = mover.tick(spread + swap(spread, axis))
    modulation, vec_float = spread[None, :6], spread[6:]
    hidden = tokens.astype(jnp.float32).reshape(1, rows, width)
    out_rows = out_grad.astype(jnp.float32).reshape(1, rows, width)
    text_mask = (jnp.arange(text.shape[1])[None, :] < text_counts[:, None])[:, None, None, :]

    def split_qkv(inputs_packed, task, query_bias, value_bias):
        low, high = task.state
        first = packed_product(inputs_packed, low)
        value = packed_product(inputs_packed, columns(high, 0, width)) + value_bias
        parts = (first[..., :width] + query_bias, first[..., width:], value)
        return tuple(split_heads(part.astype(jnp.bfloat16), heads) for part in parts)

    mod_table = modulation + vec_float[10:16][None]
    gate_one, gate_two = mod_table[:, None, 2], mod_table[:, None, 5]
    mover.finish(s_task)
    normed = modulate(hidden, mod_table[:, 0], mod_table[:, 1]).astype(jnp.bfloat16)
    frames = packed(normed.reshape(frame_count, patch_count, width))
    frames = mover.tick(frames)
    s_parts = mover.tick(split_qkv(frames, s_task, vec_float[0], vec_float[1]))
    s_mixed, s_total = attend_forward(*s_parts, None, SPATIAL)
    s_flat = mover.tick(packed(merge_heads(s_mixed)))
    s_high = columns(s_task.state[1], width, width)
    s_branch = (packed_product(s_flat, s_high) + vec_float[2]).reshape(1, rows, width)
    hidden_one = hidden + gate_one * s_branch
    moved = lax.all_to_all(
        hidden_one.astype(jnp.bfloat16).reshape(1, frame_count, patch_count, width),
        "seq",
        split_axis=2,
        concat_axis=1,
        tiled=True,
    )
    moved = mover.tick(packed(moved))
    mover.finish(t_task)
    t_parts = mover.tick(split_qkv(moved, t_task, vec_float[3], vec_float[4]))
    t_mixed, t_total = attend_forward(*t_parts, None, TEMPORAL)
    t_flat = mover.tick(packed(merge_heads(t_mixed)))
    t_high = columns(t_task.state[1], width, width)
    t_branch = (packed_product(t_flat, t_high) + vec_float[5]).astype(jnp.bfloat16)
    t_back = lax.all_to_all(t_branch, "seq", split_axis=1, concat_axis=2, tiled=True).reshape(1, rows, width)
    hidden_two = hidden_one + gate_one * t_back.astype(jnp.float32)
    cross_in = mover.tick(packed(hidden_two.astype(jnp.bfloat16)))
    mover.finish(c_task)
    c_low, c_high = c_task.state
    w_cquery, w_ckey = columns(c_low, 0, width), columns(c_low, width, width)
    w_cvalue, w_cproj = columns(c_high, 0, width), columns(c_high, width, width)
    text_packed = packed(text)
    c_query_rows = split_heads((packed_product(cross_in, w_cquery) + vec_float[6]).astype(jnp.bfloat16), heads)
    c_key = split_heads(packed_product(text_packed, w_ckey).astype(jnp.bfloat16), heads)
    c_value = split_heads((packed_product(text_packed, w_cvalue) + vec_float[7]).astype(jnp.bfloat16), heads)
    c_query_rows, c_key, c_value = mover.tick((c_query_rows, c_key, c_value))
    c_mixed, c_total = attend_forward(c_query_rows, c_key, c_value, text_mask, CROSS)
    c_flat = mover.tick(packed(merge_heads(c_mixed)))
    hidden_three = hidden_two + (packed_product(c_flat, w_cproj) + vec_float[8])
    normed_two = packed(modulate(hidden_three, mod_table[:, 3], mod_table[:, 4]).astype(jnp.bfloat16))
    normed_two = mover.tick(normed_two)
    mover.finish(i_task)
    inner_act = jnp.concatenate([packed_product(normed_two, part) for part in i_task.state], axis=-1)
    inner_act = inner_act + vec_float[16:].reshape(-1)
    gelu_out = mover.tick(jax.nn.gelu(inner_act, approximate=True).astype(jnp.bfloat16))
    mover.drain()
    w_out = o_task.state
    mlp_branch = product(gelu_out, w_out) + vec_float[9]
    hidden_four = hidden_three + gate_two * mlp_branch

    def pair(arr):
        flat = arr.reshape(-1, arr.shape[-1])
        return jnp.concatenate([flat, swap(flat, "k")], axis=0)

    def pair_packed(arr):
        flat = arr.reshape(-1, arr.shape[-1])
        other = swap(flat, "k")
        half = flat.shape[1] // 2
        return jnp.concatenate([flat, jnp.concatenate([other[:, half:], other[:, :half]], axis=1)], axis=0)

    def choose(low, high):
        return jnp.where(k == 0, low, high)

    def pair_half(low, high):
        low, high = (part.reshape(-1, part.shape[-1]) for part in (low, high))
        return jnp.concatenate([choose(low, high), swap(choose(high, low), "k")], axis=0)

    def sums_of(left, right):
        return lax.dot_general(left, right, (((0,), (0,)), ((), ())), preferred_element_type=jnp.float32).astype(
            jnp.bfloat16
        )

    grad_mlp = (out_rows * gate_two).astype(jnp.bfloat16)
    grad_gate_two = jnp.sum(out_rows * mlp_branch, axis=1)
    mlp_rows = grad_mlp.reshape(rows, width)
    sum_out = sums_of(pair(gelu_out), pair_half(mlp_rows[:, :640], mlp_rows[:, 512:]))
    bias_out = column_sum(grad_mlp)
    grad_gelu, sum_out = lax.optimization_barrier((product_back(grad_mlp, w_out), sum_out))
    own_out = mover.add(scatter_out_steps(at), sum_out)
    gelu_pull = jax.vjp(partial(jax.nn.gelu, approximate=True), inner_act)[1]
    grad_inner = mover.tick(gelu_pull(grad_gelu)[0].astype(jnp.bfloat16))
    pair_two, inner_half = pair_packed(normed_two), pair_half(grad_inner[..., :HALF], grad_inner[..., HALF:])
    sum_in = (sums_of(pair_two, inner_half[:, :width]), sums_of(pair_two, inner_half[:, width:]))
    bias_in = column_sum(grad_inner)
    norm_pull = jax.vjp(modulate, hidden_three, mod_table[:, 3], mod_table[:, 4])[1]
    in_low, in_high = i_task.state
    grad_normed = packed_back(grad_inner[..., :HALF], in_low) + packed_back(grad_inner[..., HALF:], in_high)
    grad_normed, sum_in = lax.optimization_barrier((grad_normed, sum_in))
    own_in = mover.add(scatter_steps(k), sum_in)
    grad_normed = mover.tick(grad_normed)
    grad_three, grad_shift_two, grad_scale_two = norm_pull(unpacked_float(grad_normed))
    grad_three = out_rows + grad_three
    grad_cross = grad_three.astype(jnp.bfloat16)
    bias_cproj = column_sum(grad_cross)
    grad_cmixed = unpacked(packed_back(grad_cross, w_cproj).astype(jnp.bfloat16))
    grad_cmixed = mover.tick(split_heads(grad_cmixed, heads))
    cq_grad, ck_grad, cv_grad = attend_backward(
        c_query_rows, c_key, c_value, text_mask, c_total, grad_cmixed, CROSS
    )
    grad_cquery = merge_heads(cq_grad).astype(jnp.bfloat16)
    grad_key, grad_value = merge_heads(ck_grad).astype(jnp.bfloat16), merge_heads(cv_grad).astype(jnp.bfloat16)
    grad_cquery, grad_key, grad_value = mover.tick((grad_cquery, grad_key, grad_value))
    bias_cquery = column_sum(grad_cquery)
    grad_two = grad_three + unpacked_float(packed_back(grad_cquery, w_cquery))
    bias_cvalue = column_sum(grad_value)
    text_part = unpacked_float(packed_back(grad_key, w_ckey) + packed_back(grad_value, w_cvalue))
    text_two = jnp.concatenate([text_packed[0], text_packed[0]], axis=0)
    sum_kv = sums_of(text_two, pair_half(grad_key, grad_value))
    sum_side = sums_of(choose(pair_packed(cross_in), pair_packed(c_flat)), pair_half(grad_cquery, grad_cross))
    sum_cross = (choose(sum_side, sum_kv), choose(sum_kv, sum_side))
    grad_temporal = (grad_two * gate_one).astype(jnp.bfloat16).reshape(1, frame_count, patch_count, width)
    grad_temporal, sum_cross = mover.tick((grad_temporal, sum_cross))
    own_cross = mover.add(scatter_steps(k), sum_cross)
    grad_gate_one = jnp.sum(grad_two * t_back.astype(jnp.float32), axis=1)
    grad_places = lax.all_to_all(grad_temporal, "seq", split_axis=2, concat_axis=1, tiled=True)
    bias_tproj = column_sum(grad_places)
    grad_tmixed = unpacked(packed_back(grad_places, t_high).astype(jnp.bfloat16))
    grad_tmixed = mover.tick(split_heads(grad_tmixed, heads))

    def stage_sums(grads, inputs, flat, proj_grad, task):
        query, key, value = mover.tick(tuple(merge_heads(part).astype(jnp.bfloat16) for part in grads))
        pair_in = pair_packed(inputs)
        low = sums_of(pair_in, pair_half(query, value))
        high = sums_of(choose(pair_in, pair_packed(flat)), pair_half(key, proj_grad))
        w_low, w_high = task.state
        if task is s_task:
            query, key, value, low, high = lax.optimization_barrier((query, key, value, low, high))
            owned = mover.add(scatter_steps(k), (low, high))
            mover.tick()
        back = packed_back(jnp.concatenate([query, key], axis=-1), w_low)
        back = back + packed_back(value, columns(w_high, 0, width))
        if task is t_task:
            back, low, high = lax.optimization_barrier((back, low, high))
            owned = mover.add(scatter_steps(k), (low, high))
        return owned, back, column_sum(query), column_sum(value)

    t_grads = attend_backward(*t_parts, None, t_total, grad_tmixed, TEMPORAL)
    own_t, grad_moved, bias_tquery, bias_tvalue = stage_sums(t_grads, moved, t_flat, grad_places, t_task)
    grad_moved = unpacked(grad_moved.astype(jnp.bfloat16))
    grad_moved = mover.tick(grad_moved)
    grad_frames = lax.all_to_all(grad_moved, "seq", split_axis=1, concat_axis=2, tiled=True)
    grad_one = grad_two + grad_frames.astype(jnp.float32).reshape(1, rows, width)
    grad_gate_one = grad_gate_one + jnp.sum(grad_one * s_branch, axis=1)
    grad_spatial = (grad_one * gate_one).astype(jnp.bfloat16).reshape(frame_count, patch_count, width)
    bias_sproj = column_sum(grad_spatial)
    grad_smixed = unpacked(packed_back(grad_spatial, s_high).astype(jnp.bfloat16))
    grad_smixed = mover.tick(split_heads(grad_smixed, heads))
    s_grads = attend_backward(*s_parts, None, s_total, grad_smixed, SPATIAL)
    own_s, grad_normed, bias_squery, bias_svalue = stage_sums(s_grads, frames, s_flat, grad_spatial, s_task)
    grad_normed = mover.tick(grad_normed)
    first_pull = jax.vjp(modulate, hidden, mod_table[:, 0], mod_table[:, 1])[1]
    grad_normed = mover.tick(unpacked_float(grad_normed))
    grad_zero, grad_shift_one, grad_scale_one = first_pull(grad_normed.reshape(1, rows, width))
    grad_input = grad_one + grad_zero
    grad_table = jnp.stack(
        [grad_shift_one, grad_scale_one, grad_gate_one, grad_shift_two, grad_scale_two, grad_gate_two], axis=1
    )[0]
    bias_rows = jnp.stack(
        [
            bias_squery,
            bias_svalue,
            bias_sproj,
            bias_tquery,
            bias_tvalue,
            bias_tproj,
            bias_cquery,
            bias_cvalue,
            bias_cproj,
            bias_out,
        ]
    )
    small = jnp.concatenate([bias_rows, grad_table, bias_in.reshape(4, width)], axis=0)
    small = along_z(sum_over_plane(small)[None])
    vec_grad = lax.dynamic_slice_in_dim(jnp.sum(small, axis=0), shard * ROWS, ROWS, axis=1)
    turned = jnp.stack([lax.dynamic_slice_in_dim(own_embed, (z + 4 - d) % 4, 1, axis=0)[0] for d in range(4)])
    time_grad = lax.dot_general(
        turned.astype(jnp.float32),
        small[:, 10:16].reshape(4, 6 * width),
        (((0,), (0,)), ((), ())),
        precision=HIGHEST,
        preferred_element_type=jnp.float32,
    )
    text_grad = lax.psum_scatter(text_part, "seq", scatter_dimension=2, tiled=True)
    mover.drain()
    grad_s, grad_t, grad_c = own_s.state[None], own_t.state[None], own_cross.state[None]
    return (
        hidden_four.reshape(tokens.shape),
        grad_input.reshape(tokens.shape),
        text_grad,
        time_grad,
        grad_s[..., :3456],
        grad_s[..., 3456:],
        grad_t[..., :3456],
        grad_t[..., 3456:],
        grad_c[..., :1152],
        grad_c[..., 1152:3456],
        grad_c[..., 3456:],
        own_in.state[None],
        own_out.state[None],
        vec_grad[None],
    )


def run_device(sizes, tokens, *rest):
    fits = (sizes["clip"], sizes["seq"]) == (4, 8) and tokens.shape == (1, 2, 256, 1152)
    return (fast_device if fits else per_device)(tokens, *rest)


def solution(mesh):
    placed = (
        P("clip", "seq", None, None),
        P("clip", None, None),
        P(),
        P("clip"),
        P("clip", "seq", None, None),
        P(("clip", "seq"), None),
        P(None, ("clip", "seq"), None),
        P(None, ("clip", "seq"), None),
        P(None, ("clip", "seq"), None),
        P(None, ("clip", "seq"), None),
        P(None, ("clip", "seq"), None),
        P(None, ("clip", "seq"), None),
        P(None, ("clip", "seq"), None),
        P(None, ("clip", "seq"), None),
        P(None, ("clip", "seq"), None),
        P(None, None, ("clip", "seq")),
    )
    return jax.shard_map(
        partial(run_device, dict(mesh.shape)),
        mesh=mesh,
        in_specs=placed,
        out_specs=(
            P("clip", "seq", None, None),
            P("clip", "seq", None, None),
            P("clip", None, "seq"),
            P(("clip", "seq"), None),
            P(None, ("clip", "seq"), None),
            P(None, ("clip", "seq"), None),
            P(None, ("clip", "seq"), None),
            P(None, ("clip", "seq"), None),
            P(None, ("clip", "seq"), None),
            P(None, ("clip", "seq"), None),
            P(None, ("clip", "seq"), None),
            P(None, ("clip", "seq"), None),
            P(None, ("clip", "seq"), None),
            P(None, None, ("clip", "seq")),
        ),
        check_vma=False,
    )
```
